256 devices in a mesh: img: 16 (over y, z_lo, core), txt: 16 (over z_hi, x).
Axes of the slice: x: 4, y: 4, z: 8 (z_hi: 4, z_lo: 2; z = z_hi * 2 + z_lo), core: 2. Of those that a mesh axis runs over, the one named last changes fastest.
Arguments:
- image_emb: bfloat16 [16384, 1152], P(('img', 'txt')), may hold values from -64 to 64
- report_emb: bfloat16 [16384, 1152], P(('txt', 'img')), may hold values from -64 to 64
Outputs:
- grad_images: float32 [16384, 1152], P(('img', 'txt'))
- grad_reports: float32 [16384, 1152], P(('txt', 'img'))
- row_loss: float32 [16384], P(('img', 'txt'))
The draws below stay inside these ranges and needn't reach their ends.
All inputs are finite; a program needn't handle non-finite values.
Results may differ from the reference program's by a relative error of at most 0.0078.
Values may be sent and summed in bfloat16 or wider, within the bound.
A program may use at most 64 MiB of HBM per device.

```python
import jax
import jax.numpy as jnp
from jax import lax

D = 1152
PAIRS = 16384


def pair_parts(key):
    shared = jax.random.normal(key, (PAIRS, D), jnp.float32)
    coupling = jax.random.uniform(jax.random.fold_in(key, 11), (PAIRS, 1), jnp.float32, 0.25, 0.6)
    common = jax.random.normal(jax.random.fold_in(key, 12), (1, D), jnp.float32)
    return (shared, coupling, common)


def embed_draw(key, shared, coupling, common, mix, row_lo, row_hi, col_lo, col_hi):
    own = jax.random.normal(key, (PAIRS, D), jnp.float32)
    row_scale = jnp.exp(jax.random.uniform(jax.random.fold_in(key, 21), (PAIRS, 1), jnp.float32, jnp.log(row_lo), jnp.log(row_hi)))
    col_scale = jnp.exp(jax.random.uniform(jax.random.fold_in(key, 22), (1, D), jnp.float32, jnp.log(col_lo), jnp.log(col_hi)))
    values = row_scale * col_scale * (coupling * shared + own + mix * common)
    return jnp.clip(values, -64.0, 64.0)


def draw_image_emb(key, part):
    shared, coupling, common = pair_parts(key)
    key = jax.random.fold_in(key, 1)
    return embed_draw(key, shared, coupling, common, 0.05, 3.0, 3.0, 1.0, 1.0).astype(jnp.bfloat16)


def draw_report_emb(key, part):
    shared, coupling, common = pair_parts(key)
    key = jax.random.fold_in(key, 2)
    return embed_draw(key, shared, coupling, common, 0.05, 3.0, 3.0, 1.0, 1.0).astype(jnp.bfloat16)


def setup_inputs(seed: int = 0) -> dict:
    keys = jax.random.split(jax.random.key(seed), 3)
    image_emb = draw_image_emb(jax.random.fold_in(keys[2], 71), 0)
    report_emb = draw_report_emb(jax.random.fold_in(keys[2], 71), 0)
    return {"image_emb": image_emb, "report_emb": report_emb}


logit_scale = 100.0
logit_bias = -12.0

def unit_rows(values):
    wide = values.astype(jnp.float32)
    inverse = lax.rsqrt(lax.optimization_barrier(jnp.sum(wide * wide, axis=1, keepdims=True)) + 1e-06)
    return ((wide * inverse).astype(jnp.bfloat16), wide * inverse, inverse)

def pair_tile(img_block, rep_block, img_ids, rep_ids):
    logits = logit_scale * lax.dot_general(img_block, rep_block, (((1,), (1,)), ((), ())), preferred_element_type=jnp.float32) + logit_bias
    matches = (img_ids[:, None] == rep_ids[None, :]).astype(jnp.float32)
    losses = jax.nn.softplus(-(2.0 * matches - 1.0) * logits)
    slopes = (jax.nn.sigmoid(logits) - matches).astype(jnp.bfloat16)
    g_img = logit_scale * jnp.dot(slopes, rep_block, preferred_element_type=jnp.float32)
    g_rep = logit_scale * lax.dot_general(slopes, img_block, (((0,), (0,)), ((), ())), preferred_element_type=jnp.float32)
    return (lax.optimization_barrier(jnp.sum(losses, axis=1)), g_img, g_rep)

def project_back(grads, unit_wide, inverse):
    return inverse * (grads - unit_wide * lax.optimization_barrier(jnp.sum(unit_wide * grads, axis=1, keepdims=True)))

def reference(image_emb, report_emb):
    unit_img, wide_img, inv_img = unit_rows(image_emb)
    unit_rep, wide_rep, inv_rep = unit_rows(report_emb)
    total = unit_img.shape[0]
    width = unit_img.shape[1]
    block = min(total, 1024)
    blocks = total // block
    rep_ids = jnp.arange(total, dtype=jnp.int32)

    def one_block(carry, index):
        start = (index * block).astype(jnp.int32)
        rows = lax.dynamic_slice_in_dim(unit_img, start, block, 0)
        ids = start + jnp.arange(block, dtype=jnp.int32)
        losses, g_img, g_rep = pair_tile(rows, unit_rep, ids, rep_ids)
        return (carry + g_rep, (losses, g_img))
    g_rep, (losses, g_img) = lax.scan(one_block, jnp.zeros((total, width), jnp.float32), jnp.arange(blocks, dtype=jnp.int32))
    g_img = g_img.reshape(total, width)
    row_loss = losses.reshape(total)
    return (project_back(g_img, wide_img, inv_img), project_back(g_rep, wide_rep, inv_rep), row_loss)
```

```python
import functools

import jax
import jax.numpy as jnp
from jax import lax
from jax.experimental import pallas as pl
from jax.experimental.pallas import tpu as pltpu
from jax.sharding import PartitionSpec as P

MESH = pl.DeviceIdType.MESH
F32, BF16 = jnp.float32, jnp.bfloat16
logit_scale = 100.0
logit_bias = -12.0
D = 1152
X, Y, Z, C = range(4)
SIZES = (4, 4, 8, 2)

IMG_AT = [(0, 0), (1, 0), (3, 0), (0, 1), (0, 3), (1, 1), (1, 3), (3, 1), (3, 3), (2, 0), (0, 2), (2, 1), (2, 3), (1, 2), (3, 2), (2, 2)]
IMG_POS = {o: n for n, o in enumerate(IMG_AT)}
REP_AT = [0, 1, 7, 2, 6, 3, 5, 4]
REP_POS = {o: n for n, o in enumerate(REP_AT)}
TABLE_X = sum(o[0] << (2 * n) for n, o in enumerate(IMG_AT))
TABLE_Y = sum(o[1] << (2 * n) for n, o in enumerate(IMG_AT))
TABLE_Z = sum(o << (3 * n) for n, o in enumerate(REP_AT))
JS = (2, 1, 3, 0)


def signed(table):
    return table - (1 << 32) if table >= 1 << 31 else table


def my_coords():
    i, t = lax.axis_index("img"), lax.axis_index("txt")
    x, z_hi = lax.rem(t, 4), lax.div(t, 4)
    y, z_lo, c = lax.div(i, 4), lax.rem(lax.div(i, 2), 2), lax.rem(i, 2)
    return (x, y, z_hi * 2 + z_lo, c)


def device_at(co, axis, step):
    co = list(co)
    co[axis] = lax.rem(co[axis] + step + SIZES[axis], SIZES[axis])
    x, y, z, c = co
    return (y * 4 + lax.rem(z, 2) * 2 + c, lax.div(z, 2) * 4 + x)


def rows(first, count):
    return pl.ds(first, count)


def unit_rows(ref):
    wide = ref[...].astype(F32)
    inverse = lax.rsqrt(jnp.sum(wide * wide, axis=1, keepdims=True) + 1e-06)
    return wide * inverse, inverse


def project_back(grads, unit_wide, inverse):
    return inverse * (grads - unit_wide * jnp.sum(unit_wide * grads, axis=1, keepdims=True))


def kernel(
    img_ref, rep_ref, gimg_ref, grep_ref, loss_ref,
    ibuf, rbuf, slopes, slopes_t, lacc, gr, ga1, gy,
    st_c, ld_c, st_z, ld_z, st1, ld1, st2, ld2, lb_s, lb_l, lw_s, lw_l,
    ssem, rsem,
):
    me = my_coords()
    peers = [(X, 1), (X, -1), (X, 2), (Y, 1), (Y, -1), (Y, 2), (Z, 1), (Z, -1), (C, 1)]
    barrier = pltpu.get_barrier_semaphore()
    for axis, step in peers:
        pl.semaphore_signal(barrier, inc=1, device_id=device_at(me, axis, step), device_id_type=MESH)

    unit_img, _ = unit_rows(img_ref)
    ibuf[0] = unit_img.astype(BF16)
    unit_rep, _ = unit_rows(rep_ref)
    rbuf[0, 0] = unit_rep.astype(BF16)
    lacc[...] = jnp.zeros_like(lacc)
    pl.semaphore_wait(barrier, len(peers))

    started = []
    count = [0]

    def copy(src, dst, axis, step):
        k = count[0]
        count[0] += 1
        return pltpu.make_async_remote_copy(
            src, dst, ssem.at[k], rsem.at[k], device_id=device_at(me, axis, step), device_id_type=MESH
        )

    def start(*copies):
        for one in copies:
            one.start()
            started.append(one)

    def arrive(*copies):
        for one in copies:
            one.wait_recv()

    def shift(o, axis, by):
        o = list(o)
        o[axis] = (o[axis] + by) % 4
        return tuple(o)

    def img_copy(o, part, axis, step):
        return copy(
            ibuf.at[IMG_POS[o], part], ibuf.at[IMG_POS[shift(o, axis, -step)], part], axis, step
        )

    halves = [rows(0, 32), rows(32, 32)]
    quarters = [[rows(0, 16), rows(16, 16)], [rows(32, 16), rows(48, 16)]]
    SIGNS = (1, -1)
    own = (0, 0)
    g1, g2, g3, g4 = {}, {}, {}, {}
    for h in (0, 1):
        p, q = h, 1 - h
        for s in SIGNS:
            qs = quarters[h][0 if s == 1 else 1]
            g1[h, s] = img_copy(own, halves[h], p, s)
            g2[h, s] = img_copy(shift(own, p, -s), qs, p, s)
            for j in (0, 1, 3, 2):
                g3[h, s, j] = img_copy(shift(own, p, j), halves[h], q, s)
                g4[h, s, j] = img_copy(shift(shift(own, p, j), q, -s), qs, q, s)

    chunks = [rows(0, 32), rows(32, 32)]

    def rep_copy(o, part, step):
        return copy(
            rbuf.at[REP_POS[o % 8], 0, part], rbuf.at[REP_POS[(o - step) % 8], 0, part], Z, step
        )

    zg = {}
    for s in SIGNS:
        first = 0 if s == 1 else 1
        for d in (1, 2, 3):
            for n in (first, 1 - first):
                zg[d, s, n] = rep_copy(-s * (d - 1), chunks[n], s)
        zg[4, s, first] = rep_copy(-s * 3, chunks[first], s)
    cg = {o: copy(rbuf.at[REP_POS[o], 0], rbuf.at[REP_POS[o], 1], C, 1) for o in REP_AT}

    matched = jnp.logical_and(me[Y] == lax.div(me[Z], 2), me[X] == lax.rem(me[Z], 2) * 2 + me[C])
    aside = jnp.where(matched, 0, 1 << 20)
    row_in = lax.broadcasted_iota(jnp.int32, (64, 1), 0)
    col_in = lax.broadcasted_iota(jnp.int32, (1, 128), 1)

    def tile(a, b):
        lhs = ibuf[pl.ds(a * 4, 4)].reshape(256, D)
        rhs = rbuf[pl.ds(b * 2, 2)].reshape(256, D)
        logits = logit_scale * lax.dot_general(
            lhs, rhs, (((1,), (1,)), ((), ())), preferred_element_type=F32
        ) + logit_bias
        row_ids, col_ids = [], []
        for k in range(4):
            n = (a * 4 + k) * 2
            bx = lax.rem((lax.shift_right_logical(jnp.int32(signed(TABLE_X)), n) & 3) + me[X], 4)
            by = lax.rem((lax.shift_right_logical(jnp.int32(signed(TABLE_Y)), n) & 3) + me[Y], 4)
            row_ids.append((by * 4 + bx) * 64 + aside + row_in)
        for k in range(2):
            bz = lax.rem((lax.shift_right_logical(jnp.int32(TABLE_Z), (b * 2 + k) * 3) & 7) + me[Z], 8)
            mine = (bz * 2 + me[C]) * 64
            other = (bz * 2 + 1 - me[C]) * 64
            col_ids.append(jnp.where(col_in < 64, mine + col_in, other + col_in - 64))
        matches = jnp.concatenate(row_ids, axis=0) == jnp.concatenate(col_ids, axis=1)
        e = jnp.exp(-jnp.abs(logits))
        r = 1.0 / (1.0 + e)
        sig = jnp.where(logits >= 0, r, e * r)
        losses = jnp.maximum(logits, 0.0) + jnp.log1p(e)
        losses = jnp.where(matches, losses - logits, losses)
        sl32 = jnp.where(matches, sig - 1.0, sig)
        sl = sl32.astype(BF16)
        slopes[pl.ds(a * 4, 4), :, pl.ds(pl.multiple_of(b * 256, 256), 256)] = sl.reshape(4, 64, 256)
        slopes_t[pl.ds(b * 2, 2), :, pl.ds(pl.multiple_of(a * 256, 256), 256)] = sl.T.reshape(2, 128, 256)
        lacc[pl.ds(a * 4, 4)] += (losses[:, :128] + losses[:, 128:]).reshape(4, 64, 128)

    def tiles(pairs):
        if len(pairs) == 1:
            tile(*pairs[0])
            return
        ta = sum(a << (2 * n) for n, (a, _) in enumerate(pairs))
        tb = sum(b << (2 * n) for n, (_, b) in enumerate(pairs))

        def body(n, carry):
            tile(
                lax.shift_right_logical(jnp.int32(ta), n * 2) & 3,
                lax.shift_right_logical(jnp.int32(tb), n * 2) & 3,
            )
            return carry

        lax.fori_loop(0, len(pairs), body, 0)

    for h in (0, 1):
        start(g1[h, 1], g1[h, -1])
    start(zg[1, 1, 0], zg[1, -1, 1], zg[1, 1, 1], zg[1, -1, 0])
    for h in (0, 1):
        start(g3[h, 1, 0], g3[h, -1, 0])
    start(cg[0])

    for h in (0, 1):
        for s in SIGNS:
            arrive(g1[h, s])
            start(g2[h, s])
    for n in (0, 1):
        for s in SIGNS:
            m = n if s == 1 else 1 - n
            arrive(zg[1, s, m])
            start(zg[2, s, m])
    for h in (0, 1):
        for j in (1, 3):
            start(g3[h, 1, j], g3[h, -1, j])
    start(cg[1], cg[7])
    for h in (0, 1):
        for s in SIGNS:
            arrive(g3[h, s, 0])
            start(g4[h, s, 0])
    arrive(cg[0], cg[1])
    tiles([(0, 0)])
    for h in (0, 1):
        arrive(g2[h, 1], g2[h, -1])
        start(g3[h, 1, 2], g3[h, -1, 2])
    for n in (0, 1):
        for s in SIGNS:
            m = n if s == 1 else 1 - n
            arrive(zg[2, s, m])
            start(zg[3, s, m])
    start(cg[2], cg[6])
    for h in (0, 1):
        for j in (1, 3):
            for s in SIGNS:
                arrive(g3[h, s, j])
                start(g4[h, s, j])
    arrive(cg[7], cg[2])
    tiles([(0, 1), (1, 0), (1, 1)])
    for s in SIGNS:
        m = 0 if s == 1 else 1
        arrive(zg[3, s, m])
        start(zg[4, s, m])
    for s in SIGNS:
        m = 1 if s == 1 else 0
        arrive(zg[3, s, m])
    start(cg[3], cg[5])
    for h in (0, 1):
        for s in SIGNS:
            arrive(g3[h, s, 2])
            start(g4[h, s, 2])
    for h in (0, 1):
        arrive(g4[h, 1, 0], g4[h, -1, 0])
    arrive(g4[1, 1, 1], g4[1, -1, 1])
    arrive(cg[6], cg[3])
    tiles([(0, 2), (1, 2), (2, 0), (2, 1), (2, 2)])
    arrive(zg[4, 1, 0], zg[4, -1, 1])
    start(cg[4])
    for h in (0, 1):
        for j in (1, 3, 2):
            if (h, j) != (1, 1):
                arrive(g4[h, 1, j], g4[h, -1, j])
    tiles([(3, 0), (3, 1), (3, 2)])
    arrive(cg[5], cg[4])
    tiles([(0, 3), (1, 3), (2, 3), (3, 3)])

    def at(h, j, dq):
        return (j, dq % 4) if h == 0 else (dq % 4, j)

    def img_terms(pieces):
        lhs = jnp.concatenate([slopes[IMG_POS[at(*n)], halves[n[0]]] for n in pieces], axis=0)
        rhs = rbuf[...].reshape(1024, D)
        return logit_scale * jnp.dot(lhs, rhs, preferred_element_type=F32)

    def rep_terms(offsets):
        lhs = jnp.concatenate([slopes_t[REP_POS[o]] for o in offsets], axis=0)
        rhs = ibuf[...].reshape(1024, D)
        out = logit_scale * jnp.dot(lhs, rhs, preferred_element_type=F32)
        for n, o in enumerate(offsets):
            gr[REP_POS[o]] = out[n * 128 : n * 128 + 64]
            st_c[REP_POS[o]] = out[n * 128 + 64 : n * 128 + 128].astype(BF16)

    r1, r2, rz, lx, ly = {}, {}, {}, {}, {}
    for h in (0, 1):
        p, q = h, 1 - h
        for n, s in enumerate(SIGNS):
            for slot in range(3):
                groups = [rows(0, 4)] if slot == 0 else [rows(0, 3), rows(3, 1)]
                for g, part in enumerate(groups):
                    r1[h, s, slot, g] = copy(st1.at[h, n, slot, part], ld1.at[h, n, slot, part], q, s)
                r2[h, s, slot] = copy(st2.at[h, n, slot], ld2.at[h, n, slot], p, s)
    for n, s in enumerate(SIGNS):
        for slot in range(7):
            rz[s, slot] = copy(st_z.at[n, slot], ld_z.at[n, slot], Z, s)
    cr = {o: copy(st_c.at[REP_POS[o]], ld_c.at[REP_POS[o]], C, 1) for o in REP_AT}
    for d, step in ((1, 1), (2, 2), (3, -1)):
        lx[d] = copy(lb_s.at[d], lb_l.at[d], X, step)
        ly[d] = copy(lw_s, lw_l.at[d], Y, step)

    def first_out(h, out, at_row):
        for k in range(4):
            for n in (0, 1):
                st1[h, n, 0, k] = out[at_row + k * 32 + n * 16 : at_row + k * 32 + n * 16 + 16].astype(BF16)

    def second_out(h, out):
        for n in (0, 1):
            for k in range(4):
                base = (n * 4 + k) * 32
                quarter = [out[base : base + 16], out[base + 16 : base + 32]]
                st1[h, n, 1, k] = quarter[1 - n].astype(BF16)
                ga1[h, n, k] = quarter[n]

    def carry_on(h, g):
        for n, s in enumerate(SIGNS):
            if g == 0:
                arrive(r1[h, s, 0, 0])
            for k in (0, 1, 2) if g == 0 else (3,):
                st1[h, n, 2, k] = (ga1[h, n, k] + ld1[h, n, 0, k].astype(F32)).astype(BF16)
            start(r1[h, s, 2, g])

    def paired(o, part):
        return gr[REP_POS[o % 8], part] + ld_c[REP_POS[o % 8], part].astype(F32)

    def z_send(slot):
        d = 4 - (slot + 1) // 2
        for n, s in enumerate(SIGNS):
            carried = slot % 2 == 0
            part = chunks[n] if carried else chunks[1 - n]
            term = paired(s * d, part)
            if slot >= 2:
                arrive(rz[s, slot - 2])
                term = term + ld_z[n, slot - 2].astype(F32)
            st_z[n, slot] = term.astype(BF16)
            start(rz[s, slot])

    out = img_terms([(h, j, 2) for h in (0, 1) for j in JS])
    for h in (0, 1):
        first_out(h, out, h * 128)
        start(r1[h, 1, 0, 0], r1[h, -1, 0, 0])
    rep_terms([4, 0])
    start(cr[4], cr[0])
    for h in (0, 1):
        second_out(h, img_terms([(h, j, s) for s in SIGNS for j in JS]))
        for s in SIGNS:
            start(r1[h, s, 1, 0])
        if h == 0:
            arrive(cr[4])
            z_send(0)
    rep_terms([3, 5])
    start(cr[3], cr[5])
    for h in (0, 1):
        carry_on(h, 0)
        start(r1[h, 1, 1, 1], r1[h, -1, 1, 1])
    rep_terms([2, 6])
    start(cr[2], cr[6])
    arrive(cr[3], cr[5])
    z_send(1)
    z_send(2)
    for h in (0, 1):
        carry_on(h, 1)
    rep_terms([1, 7])
    start(cr[1], cr[7])
    arrive(cr[2], cr[6])
    z_send(3)
    out = img_terms([(h, j, 0) for h in (0, 1) for j in JS])
    for h in (0, 1):
        for k in range(4):
            gy[h, k] = out[(h * 4 + k) * 32 : (h * 4 + k) * 32 + 32]

    lb_s[...] = jnp.zeros_like(lb_s)
    for k in range(8):
        line = jnp.sum(lacc[2 * k : 2 * k + 2].reshape(128, 128).T, axis=0, keepdims=True)
        for n in (0, 1):
            dx, dy = IMG_AT[2 * k + n]
            lb_s[dx, dy : dy + 1, :] = line if n == 0 else pltpu.roll(line, 64, 1)
    start(lx[1], lx[2], lx[3])
    z_send(4)

    arrive(lx[1], lx[2], lx[3])
    lw_s[...] = lb_s[0] + lb_l[1] + lb_l[2] + lb_l[3]
    start(ly[1], ly[2], ly[3])
    arrive(cr[1], cr[7])
    z_send(5)

    def line_sum(h, k, n):
        total = gy[h, k, n * 16 : n * 16 + 16]
        total = total + ld1[h, n, 2, k].astype(F32)
        return total + ld1[h, 1 - n, 1, k].astype(F32)

    for h in (0, 1):
        for s in SIGNS:
            arrive(r1[h, s, 1, 0], r1[h, s, 2, 0])
        for n, s in enumerate(SIGNS):
            st2[h, n, 0] = line_sum(h, 0, n).astype(BF16)
            start(r2[h, s, 0])
    for h in (0, 1):
        for n, s in enumerate(SIGNS):
            st2[h, n, 1] = line_sum(h, 1 + n, 1 - n).astype(BF16)
            start(r2[h, s, 1])
    z_send(6)
    for h in (0, 1):
        for n, s in enumerate(SIGNS):
            arrive(r2[h, s, 0])
            st2[h, n, 2] = (line_sum(h, 1 + n, n) + ld2[h, n, 0].astype(F32)).astype(BF16)
            start(r2[h, s, 2])

    arrive(ly[1], ly[2], ly[3])
    loss = lw_s[0:1, :]
    for d in (1, 2, 3):
        loss = loss + lw_l[d, d : d + 1, :]
    loss_ref[...] = jnp.broadcast_to(loss, loss_ref.shape)

    for n, s in enumerate(SIGNS):
        arrive(rz[s, 5], rz[s, 6])
    arrive(cr[0])
    unit_rep, inv_rep = unit_rows(rep_ref)
    halves_rep = []
    for n in (0, 1):
        total = paired(0, chunks[n]) + ld_z[n, 6].astype(F32) + ld_z[1 - n, 5].astype(F32)
        halves_rep.append(total)
    grep_ref[...] = project_back(jnp.concatenate(halves_rep, axis=0), unit_rep, inv_rep)

    quarter_sums = []
    for h in (0, 1):
        for s in SIGNS:
            arrive(r1[h, s, 1, 1], r1[h, s, 2, 1], r2[h, s, 1], r2[h, s, 2])
        for n in (0, 1):
            quarter_sums.append(
                line_sum(h, 3, n) + ld2[h, n, 2].astype(F32) + ld2[h, 1 - n, 1].astype(F32)
            )
    unit_img, inv_img = unit_rows(img_ref)
    gimg_ref[...] = project_back(jnp.concatenate(quarter_sums, axis=0), unit_img, inv_img)
    for one in started:
        one.wait_send()


COPIES = 40 + 14 + 8 + 20 + 12 + 14 + 8 + 6


def on_device(image_emb, report_emb):
    vmem = pl.BlockSpec(memory_space=pltpu.VMEM)
    gimg, grep, loss = pl.pallas_call(
        kernel,
        out_shape=(
            jax.ShapeDtypeStruct((64, D), F32),
            jax.ShapeDtypeStruct((64, D), F32),
            jax.ShapeDtypeStruct((8, 128), F32),
        ),
        in_specs=[vmem, vmem],
        out_specs=(vmem, vmem, vmem),
        scratch_shapes=[
            pltpu.VMEM((16, 64, D), BF16),
            pltpu.VMEM((8, 2, 64, D), BF16),
            pltpu.VMEM((16, 64, 1024), BF16),
            pltpu.VMEM((8, 128, 1024), BF16),
            pltpu.VMEM((16, 64, 128), F32),
            pltpu.VMEM((8, 64, D), F32),
            pltpu.VMEM((2, 2, 4, 16, D), F32),
            pltpu.VMEM((2, 4, 32, D), F32),
            pltpu.VMEM((8, 64, D), BF16),
            pltpu.VMEM((8, 64, D), BF16),
            pltpu.VMEM((2, 7, 32, D), BF16),
            pltpu.VMEM((2, 7, 32, D), BF16),
            pltpu.VMEM((2, 2, 3, 4, 16, D), BF16),
            pltpu.VMEM((2, 2, 3, 4, 16, D), BF16),
            pltpu.VMEM((2, 2, 3, 16, D), BF16),
            pltpu.VMEM((2, 2, 3, 16, D), BF16),
            pltpu.VMEM((4, 8, 128), F32),
            pltpu.VMEM((4, 8, 128), F32),
            pltpu.VMEM((8, 128), F32),
            pltpu.VMEM((4, 8, 128), F32),
            pltpu.SemaphoreType.DMA((COPIES,)),
            pltpu.SemaphoreType.DMA((COPIES,)),
        ],
        compiler_params=pltpu.CompilerParams(
            collective_id=0, has_side_effects=True, vmem_limit_bytes=56 * 2**20
        ),
        cost_estimate=pl.CostEstimate(
            flops=3 * 2 * 1024 * 1024 * D, bytes_accessed=900000, transcendentals=3 * 1024 * 1024
        ),
    )(image_emb, report_emb)
    return gimg, grep, loss[0, :64]


def solution(mesh):
    in_specs = (P(("img", "txt"), None), P(("txt", "img"), None))
    out_specs = (P(("img", "txt"), None), P(("txt", "img"), None), P(("img", "txt")))
    return jax.shard_map(
        on_device, mesh=mesh, in_specs=in_specs, out_specs=out_specs, check_vma=False
    )
```

```python
import functools

import jax
import jax.numpy as jnp
from jax import lax
from jax.experimental import pallas as pl
from jax.experimental.pallas import tpu as pltpu
from jax.sharding import PartitionSpec as P

MESH = pl.DeviceIdType.MESH
F32, BF16 = jnp.float32, jnp.bfloat16
LOG2E, LN2 = 1.4426950408889634, 0.6931471805599453
logit_scale = 100.0
logit_bias = -12.0
D = 1152
X, Y, Z, C = range(4)
SIZES = (4, 4, 8, 2)
SIGNS = (1, -1)

IMG_AT = [(0, 0), (1, 0), (3, 0), (0, 1), (0, 3), (1, 1), (1, 3), (3, 1), (3, 3), (2, 0), (0, 2), (2, 1), (2, 3), (1, 2), (3, 2), (2, 2)]
REP_AT = [0, 1, 7, 2, 6, 3, 5, 4]
IMG_POS = {o: n for n, o in enumerate(IMG_AT)}
REP_POS = {o: n for n, o in enumerate(REP_AT)}
JS = (2, 1, 3, 0)
TILES = [(0, 4, 0, 4), (4, 4, 0, 4), (0, 8, 4, 2), (8, 4, 0, 6), (0, 12, 6, 2), (12, 4, 0, 8)]


def shift(o, axis, by):
    o = list(o)
    o[axis] = (o[axis] + by) % 4
    return tuple(o)


def at(h, j, dq):
    return (j, dq % 4) if h == 0 else (dq % 4, j)


def z_chunks(s):
    return (0, 1, 2, 3) if s == 1 else (2, 3, 0, 1)


def plan():
    steps = []

    def add(name, axis, step, rows, needs):
        steps.append((name, axis, step, rows, list(dict.fromkeys(needs))))
        return [name]

    img = {((0, 0), h, u): [] for h in (0, 1) for u in (0, 1)}
    for h in (0, 1):
        p, q = h, 1 - h
        for u in (0, 1):
            for s in SIGNS:
                img[shift((0, 0), p, -s), h, u] = add(("g1", h, s, u), p, s, 16, [])
        for n, s in enumerate(SIGNS):
            src = shift((0, 0), p, -s)
            img[shift(src, p, -s), h, n] = add(("g2", h, s), p, s, 16, img[src, h, n])
        for j in (0, 1, 3, 2):
            line = shift((0, 0), p, j)
            for u in (0, 1):
                for s in SIGNS:
                    img[shift(line, q, -s), h, u] = add(("g3", h, s, j, u), q, s, 16, img[line, h, u])
            for n, s in enumerate(SIGNS):
                src = shift(line, q, -s)
                img[shift(src, q, -s), h, n] = add(("g4", h, s, j), q, s, 16, img[src, h, n])
    rep = {(0, c): [] for c in range(4)}
    for s in SIGNS:
        for d in (1, 2, 3, 4):
            for c in z_chunks(s)[: 4 if d < 4 else 2]:
                rep[-s * d % 8, c] = add(("z", d, s, c), Z, s, 16, rep[-s * (d - 1) % 8, c])
    whole = {}
    for o in REP_AT:
        mine = [n for c in range(4) for n in rep[o, c]]
        whole[o] = mine + add(("cg", o), C, 1, 64, mine)
    cover = {}
    for i, ni, r, nr in TILES:
        needs = [n for k in range(i, i + ni) for h in (0, 1) for u in (0, 1) for n in img[IMG_AT[k], h, u]]
        needs += [n for k in range(r, r + nr) for n in whole[REP_AT[k]]]
        add(("tile", i, ni, r, nr), None, 0, ni * nr, needs)
        for k in range(i, i + ni):
            for m in range(r, r + nr):
                cover[k, m] = ("tile", i, ni, r, nr)
    img_tiles = lambda blocks: [cover[IMG_POS[o], m] for o in blocks for m in range(8)]
    rep_tiles = lambda blocks: [cover[k, REP_POS[o]] for o in blocks for k in range(16)]
    add("ig2", None, 0, 256, img_tiles([at(h, j, 2) for h in (0, 1) for j in JS]))
    for h in (0, 1):
        add(("ig1", h), None, 0, 256, img_tiles([at(h, j, s) for s in SIGNS for j in JS]))
    add("ig0", None, 0, 256, img_tiles([at(h, j, 0) for h in (0, 1) for j in JS]))
    for d in (4, 3, 2, 1):
        add(("rg", d), None, 0, 256, rep_tiles([d, 0] if d == 4 else [d, 8 - d]))
    for d in (4, 3, 2, 1, 0):
        for o in (d, 8 - d) if d in (1, 2, 3) else (d,):
            add(("cr", o), C, 1, 64, [("rg", d or 4)])
    for s in SIGNS:
        order = z_chunks(s)
        for c in order[:2]:
            add(("rz", 4, s, c), Z, s, 16, [("cr", 4)])
        for d in (3, 2, 1):
            for c in order[2:] + order[:2]:
                before = [] if d == 3 and c in order[2:] else [("rz", d + 1, s, c)]
                add(("rz", d, s, c), Z, s, 16, [("cr", s * d % 8)] + before)
    for h in (0, 1):
        p, q = h, 1 - h
        for s in SIGNS:
            for j in JS:
                add(("r1", h, s, 0, j), q, s, 16, ["ig2"])
                add(("r1", h, s, 1, j), q, s, 16, [("ig1", h)])
                add(("r1", h, s, 2, j), q, s, 16, [("ig1", h), ("r1", h, s, 0, j)])
        for n, s in enumerate(SIGNS):
            line = lambda j, u: ["ig0", ("r1", h, SIGNS[u], 2, j), ("r1", h, SIGNS[1 - u], 1, j)]
            add(("r2", h, s, 0), p, s, 16, line(2, n))
            add(("r2", h, s, 1), p, s, 16, line(s % 4, 1 - n))
            add(("r2", h, s, 2), p, s, 16, line(s % 4, n) + [("r2", h, s, 0)])
    add("loss", None, 0, 0, list(cover.values()))
    for d in (1, 2, 3):
        add(("lx", d), X, d, 2, ["loss"])
    for d in (1, 2, 3):
        add(("ly", d), Y, d, 2, [("lx", e) for e in (1, 2, 3)])
    add("out_rep", None, 0, 0, [("cr", 0)] + [("rz", 1, s, c) for s in SIGNS for c in range(4)])
    lines = [("r1", h, s, k, 0) for h in (0, 1) for s in SIGNS for k in (1, 2)]
    add("out_img", None, 0, 0, ["ig0"] + lines + [("r2", h, s, k) for h in (0, 1) for s in SIGNS for k in (1, 2)])
    add("out_loss", None, 0, 0, [("ly", d) for d in (1, 2, 3)])
    return steps


ORDER = [
    60, 61, 74, 75, 0, 3, 30, 33, 62, 76, 1, 2, 32, 31, 6, 9, 36, 39, 88, 63, 77, 38, 37, 8, 7, 64, 78, 4, 5, 34, 35,
    15, 18, 48, 45, 44, 49, 14, 19, 65, 79, 42, 51, 12, 21, 66, 80, 40, 41, 10, 11, 67, 90, 81, 89, 50, 43, 20, 13,
    68, 82, 54, 57, 24, 27, 69, 83, 52, 55, 22, 17, 70, 84, 56, 47, 26, 25, 71, 92, 85, 91, 46, 53, 16, 23, 72, 86,
    96, 73, 87, 97, 28, 29, 58, 59, 93, 94, 98, 95, 99, 101, 100, 106, 110, 117, 102, 146, 158, 176, 118, 119, 132,
    133, 188, 149, 152, 161, 164, 179, 182, 191, 194, 155, 167, 185, 197, 107, 111, 112, 103, 147, 148, 159, 120, 121,
    122, 134, 135, 136, 160, 150, 162, 151, 104, 123, 137, 177, 178, 189, 190, 153, 163, 154, 165, 166, 180, 192, 108,
    113, 114, 181, 183, 193, 195, 156, 157, 168, 169, 184, 105, 124, 125, 126, 138, 139, 140, 170, 173, 196, 200, 203,
    171, 127, 198, 206, 207, 208, 209, 141, 174, 186, 109, 115, 116, 187, 199, 201, 204, 175, 202, 128, 129, 172, 142,
    143, 205, 130, 144, 210, 211, 212, 131, 145, 214, 215, 213,
]


def my_coords():
    i, t = lax.axis_index("img"), lax.axis_index("txt")
    x, z_hi = lax.rem(t, 4), lax.div(t, 4)
    y, z_lo, c = lax.div(i, 4), lax.rem(lax.div(i, 2), 2), lax.rem(i, 2)
    return (x, y, z_hi * 2 + z_lo, c)


def device_at(co, axis, step):
    co = list(co)
    co[axis] = lax.rem(co[axis] + step + SIZES[axis], SIZES[axis])
    x, y, z, c = co
    return (y * 4 + lax.rem(z, 2) * 2 + c, lax.div(z, 2) * 4 + x)


def unit_rows(ref):
    wide = ref[...].astype(F32)
    inverse = lax.rsqrt(jnp.sum(wide * wide, axis=1, keepdims=True) + 1e-06)
    return wide * inverse, inverse


def project_back(grads, unit_wide, inverse):
    return inverse * (grads - unit_wide * jnp.sum(unit_wide * grads, axis=1, keepdims=True))


def kernel(
    img_ref, rep_ref, gimg_ref, grep_ref, loss_ref,
    own_img, own_rep, ibuf, rbuf, slopes, above, below, gr, ga1, gy,
    st_c, ld_c, st_z, ld_z, st1, ld1, st2, ld2, lb_s, lb_l, lw_s, lw_l,
    ssem, rsem, own_sem,
):
    me = my_coords()
    peers = [(X, 1), (X, -1), (X, 2), (Y, 1), (Y, -1), (Y, 2), (Z, 1), (Z, -1), (C, 1)]
    barrier = pltpu.get_barrier_semaphore()
    for axis, step in peers:
        pl.semaphore_signal(barrier, inc=1, device_id=device_at(me, axis, step), device_id_type=MESH)
    loads = [
        pltpu.make_async_copy(img_ref, own_img, own_sem.at[0]),
        pltpu.make_async_copy(rep_ref, own_rep, own_sem.at[1]),
    ]
    for load in loads:
        load.start()
    above[...] = jnp.zeros_like(above)
    below[...] = jnp.zeros_like(below)
    lb_s[...] = jnp.zeros_like(lb_s)
    for load in loads:
        load.wait()
    ibuf[0] = unit_rows(own_img)[0].astype(BF16)
    rbuf[0, 0] = unit_rows(own_rep)[0].astype(BF16)
    pl.semaphore_wait(barrier, len(peers))

    def quarter(n, count=1):
        return pl.ds(n * 16, count * 16)

    matched = jnp.logical_and(me[Y] == lax.div(me[Z], 2), me[X] == lax.rem(me[Z], 2) * 2 + me[C])
    aside = jnp.where(matched, 0, 1 << 20)
    row_in = lax.broadcasted_iota(jnp.int32, (64, 1), 0)
    col_in = lax.broadcasted_iota(jnp.int32, (1, 128), 1)

    def tile(i, ni, r, nr):
        m = ni * 64
        lhs = ibuf[i : i + ni].reshape(m, D)
        rhs = rbuf[r : r + nr].reshape(nr * 128, D)
        dots = lax.dot_general(lhs, rhs, (((1,), (1,)), ((), ())), preferred_element_type=F32)
        row_ids = []
        for dx, dy in IMG_AT[i : i + ni]:
            block = lax.rem(me[Y] + dy, 4) * 4 + lax.rem(me[X] + dx, 4)
            row_ids.append(block * 64 + aside + row_in)
        row_ids = jnp.concatenate(row_ids, axis=0)
        high = above[i : i + ni].reshape(m, 128)
        low = below[i : i + ni].reshape(m, 128)
        for k in range(nr):
            bz = lax.rem(me[Z] + REP_AT[r + k], 8) * 2
            mine, other = (bz + me[C]) * 64, (bz + 1 - me[C]) * 64
            col_ids = jnp.where(col_in < 64, mine + col_in, other + col_in - 64)
            sign = jnp.where(row_ids == col_ids, -1.0, 1.0)
            bits = (dots[:, k * 128 : k * 128 + 128] * (logit_scale * LOG2E) + logit_bias * LOG2E) * sign
            e = jnp.exp2(-jnp.abs(bits))
            one_e = 1.0 + e
            inverse = 1.0 / one_e
            slope = jnp.where(bits >= 0, inverse, e * inverse) * sign
            slopes[i : i + ni, :, (r + k) * 128 : (r + k) * 128 + 128] = slope.astype(BF16).reshape(ni, 64, 128)
            high = high + jnp.maximum(bits, 0.0)
            low = low * one_e + e
        above[i : i + ni] = high.reshape(ni, 64, 128)
        below[i : i + ni] = low.reshape(ni, 64, 128)

    def img_terms(pieces):
        lhs = jnp.concatenate([slopes[IMG_POS[at(*n)], quarter(2 * n[0], 2)] for n in pieces], axis=0)
        return logit_scale * jnp.dot(lhs, rbuf[...].reshape(1024, D), preferred_element_type=F32)

    def rep_terms(offsets):
        cols = [slopes[:, :, REP_POS[o] * 128 : REP_POS[o] * 128 + 128].reshape(1024, 128) for o in offsets]
        out = logit_scale * lax.dot_general(
            jnp.concatenate(cols, axis=1), ibuf[...].reshape(1024, D), (((0,), (0,)), ((), ())),
            preferred_element_type=F32,
        )
        for n, o in enumerate(offsets):
            gr[REP_POS[o]] = out[n * 128 : n * 128 + 64]
            st_c[REP_POS[o]] = out[n * 128 + 64 : n * 128 + 128].astype(BF16)

    def far_terms():
        out = img_terms([(h, j, 2) for h in (0, 1) for j in JS])
        for h in (0, 1):
            for k in range(4):
                for n in (0, 1):
                    base = (h * 4 + k) * 32 + n * 16
                    st1[h, n, 0, k] = out[base : base + 16].astype(BF16)

    def near_terms(h):
        out = img_terms([(h, j, s) for s in SIGNS for j in JS])
        for n in (0, 1):
            for k in range(4):
                base = (n * 4 + k) * 32
                quarters = [out[base : base + 16], out[base + 16 : base + 32]]
                st1[h, n, 1, k] = quarters[1 - n].astype(BF16)
                ga1[h, n, k] = quarters[n]

    def line_terms():
        out = img_terms([(h, j, 0) for h in (0, 1) for j in JS])
        for h in (0, 1):
            for k in range(4):
                gy[h, k] = out[(h * 4 + k) * 32 : (h * 4 + k) * 32 + 32]

    def line_sum(h, j, u):
        k = JS.index(j)
        total = gy[h, k, quarter(u)] + ld1[h, u, 2, k].astype(F32)
        return total + ld1[h, 1 - u, 1, k].astype(F32)

    def paired(o, c):
        return gr[REP_POS[o % 8], quarter(c)] + ld_c[REP_POS[o % 8], quarter(c)].astype(F32)

    def losses():
        for k in range(8):
            wide = above[2 * k : 2 * k + 2] * LN2 + jnp.log1p(below[2 * k : 2 * k + 2])
            line = jnp.sum(wide.reshape(128, 128).T, axis=0, keepdims=True)
            for n in (0, 1):
                dx, dy = IMG_AT[2 * k + n]
                lb_s[dx, dy : dy + 1, :] = line if n == 0 else pltpu.roll(line, 64, 1)

    def x_losses():
        lw_s[...] = lb_s[0] + lb_l[1] + lb_l[2] + lb_l[3]

    def out_rep():
        parts = [paired(0, c) + ld_z[0, 0, c].astype(F32) + ld_z[1, 0, c].astype(F32) for c in range(4)]
        unit, inverse = unit_rows(own_rep)
        grep_ref[...] = project_back(jnp.concatenate(parts, axis=0), unit, inverse)

    def out_img():
        parts = [
            line_sum(h, 0, u) + ld2[h, u, 2].astype(F32) + ld2[h, 1 - u, 1].astype(F32)
            for h in (0, 1)
            for u in (0, 1)
        ]
        unit, inverse = unit_rows(own_img)
        gimg_ref[...] = project_back(jnp.concatenate(parts, axis=0), unit, inverse)

    def out_loss():
        loss = lw_s[0:1, :]
        for d in (1, 2, 3):
            loss = loss + lw_l[d, d : d + 1, :]
        loss_ref[...] = jnp.broadcast_to(loss, loss_ref.shape)

    compute = {
        "tile": tile, "ig2": far_terms, "ig1": near_terms, "ig0": line_terms,
        "rg": lambda d: rep_terms([4, 0] if d == 4 else [d, 8 - d]),
        "loss": losses, "out_rep": out_rep, "out_img": out_img, "out_loss": out_loss,
    }

    def img_ends(o, part, axis, s):
        return ibuf.at[IMG_POS[o], part], ibuf.at[IMG_POS[shift(o, axis, -s)], part]

    def ends(name):
        kind, a = name[0], name[1:]
        if kind == "g1":
            h, s, u = a
            return img_ends((0, 0), quarter(2 * h + u), h, s)
        if kind == "g2":
            h, s = a
            return img_ends(shift((0, 0), h, -s), quarter(2 * h + SIGNS.index(s)), h, s)
        if kind == "g3":
            h, s, j, u = a
            return img_ends(at(h, j, 0), quarter(2 * h + u), 1 - h, s)
        if kind == "g4":
            h, s, j = a
            return img_ends(at(h, j, -s), quarter(2 * h + SIGNS.index(s)), 1 - h, s)
        if kind == "z":
            d, s, c = a
            return (
                rbuf.at[REP_POS[-s * (d - 1) % 8], 0, quarter(c)],
                rbuf.at[REP_POS[-s * d % 8], 0, quarter(c)],
            )
        if kind == "cg":
            return rbuf.at[REP_POS[a[0]], 0], rbuf.at[REP_POS[a[0]], 1]
        if kind == "cr":
            return st_c.at[REP_POS[a[0]]], ld_c.at[REP_POS[a[0]]]
        if kind == "rz":
            d, s, c = a
            return st_z.at[SIGNS.index(s), d - 1, c], ld_z.at[SIGNS.index(s), d - 1, c]
        if kind == "r1":
            h, s, slot, j = a
            where = (h, SIGNS.index(s), slot, JS.index(j))
            return st1.at[where], ld1.at[where]
        if kind == "r2":
            h, s, slot = a
            return st2.at[h, SIGNS.index(s), slot], ld2.at[h, SIGNS.index(s), slot]
        if kind == "lx":
            return lb_s.at[a[0]], lb_l.at[a[0]]
        return lw_s, lw_l.at[a[0]]

    def prepare(name):
        kind, a = name[0], name[1:]
        if kind == "rz":
            d, s, c = a
            n = SIGNS.index(s)
            term = paired(s * d, c)
            if d < 3 or (d == 3 and c in z_chunks(s)[:2]):
                term = term + ld_z[n, d, c].astype(F32)
            st_z[n, d - 1, c] = term.astype(BF16)
        if kind == "r1" and a[2] == 2:
            h, s, _, j = a
            n, k = SIGNS.index(s), JS.index(j)
            st1[h, n, 2, k] = (ga1[h, n, k] + ld1[h, n, 0, k].astype(F32)).astype(BF16)
        if kind == "r2":
            h, s, slot = a
            n = SIGNS.index(s)
            term = line_sum(h, 2 if slot == 0 else s % 4, 1 - n if slot == 1 else n)
            if slot == 2:
                term = term + ld2[h, n, 0].astype(F32)
            st2[h, n, slot] = term.astype(BF16)
        if name == ("ly", 1):
            x_losses()

    steps = plan()
    copies = {}
    for name, axis, step, _, _ in steps:
        if axis is not None:
            k = len(copies)
            src, dst = ends(name)
            copies[name] = pltpu.make_async_remote_copy(
                src, dst, ssem.at[k], rsem.at[k], device_id=device_at(me, axis, step), device_id_type=MESH
            )
    arrived = set()
    for n in ORDER:
        name, axis, _, _, needs = steps[n]
        for need in needs:
            if need in copies and need not in arrived:
                copies[need].wait_recv()
                arrived.add(need)
        if axis is None:
            args = () if isinstance(name, str) else name[1:]
            compute[name if isinstance(name, str) else name[0]](*args)
        else:
            prepare(name)
            copies[name].start()
    for copy in copies.values():
        copy.wait_send()


def finish(gimg, grep, loss, out_img, out_rep, out_loss, sem):
    stores = [pltpu.make_async_copy(gimg, out_img, sem.at[0]), pltpu.make_async_copy(grep, out_rep, sem.at[1])]
    for store in stores:
        store.start()
    out_loss[...] = loss[0, :64]
    for store in stores:
        store.wait()


COPIES = sum(step[1] is not None for step in plan())


def on_device(image_emb, report_emb):
    vmem = pl.BlockSpec(memory_space=pltpu.VMEM)
    hbm = pl.BlockSpec(memory_space=pl.ANY)
    sums = (
        jax.ShapeDtypeStruct((64, D), F32),
        jax.ShapeDtypeStruct((64, D), F32),
        jax.ShapeDtypeStruct((8, 128), F32),
    )
    gimg, grep, loss = pl.pallas_call(
        kernel,
        out_shape=(pltpu.VMEM((64, D), F32), pltpu.VMEM((64, D), F32), pltpu.VMEM((8, 128), F32)),
        in_specs=[pl.BlockSpec(memory_space=pltpu.HBM)] * 2,
        out_specs=(vmem, vmem, vmem),
        scratch_shapes=[
            pltpu.VMEM((64, D), BF16),
            pltpu.VMEM((64, D), BF16),
            pltpu.VMEM((16, 64, D), BF16),
            pltpu.VMEM((8, 2, 64, D), BF16),
            pltpu.VMEM((16, 64, 1024), BF16),
            pltpu.VMEM((16, 64, 128), F32),
            pltpu.VMEM((16, 64, 128), F32),
            pltpu.VMEM((8, 64, D), F32),
            pltpu.VMEM((2, 2, 4, 16, D), F32),
            pltpu.VMEM((2, 4, 32, D), F32),
            pltpu.VMEM((8, 64, D), BF16),
            pltpu.VMEM((8, 64, D), BF16),
            pltpu.VMEM((2, 4, 4, 16, D), BF16),
            pltpu.VMEM((2, 4, 4, 16, D), BF16),
            pltpu.VMEM((2, 2, 3, 4, 16, D), BF16),
            pltpu.VMEM((2, 2, 3, 4, 16, D), BF16),
            pltpu.VMEM((2, 2, 3, 16, D), BF16),
            pltpu.VMEM((2, 2, 3, 16, D), BF16),
            pltpu.VMEM((4, 8, 128), F32),
            pltpu.VMEM((4, 8, 128), F32),
            pltpu.VMEM((8, 128), F32),
            pltpu.VMEM((4, 8, 128), F32),
            pltpu.SemaphoreType.DMA((COPIES,)),
            pltpu.SemaphoreType.DMA((COPIES,)),
            pltpu.SemaphoreType.DMA((2,)),
        ],
        compiler_params=pltpu.CompilerParams(
            collective_id=0, has_side_effects=True, vmem_limit_bytes=40 * 2**20
        ),
        cost_estimate=pl.CostEstimate(
            flops=3 * 2 * 1024 * 1024 * D, bytes_accessed=900000, transcendentals=3 * 1024 * 1024
        ),
    )(pltpu.with_memory_space_constraint(image_emb, pltpu.HBM), pltpu.with_memory_space_constraint(report_emb, pltpu.HBM))
    return pl.pallas_call(
        finish,
        out_shape=sums[:2] + (jax.ShapeDtypeStruct((64,), F32),),
        in_specs=[vmem, vmem, vmem],
        out_specs=(hbm, hbm, vmem),
        scratch_shapes=[pltpu.SemaphoreType.DMA((2,))],
        compiler_params=pltpu.CompilerParams(vmem_limit_bytes=8 * 2**20),
    )(gimg, grep, loss)


def solution(mesh):
    in_specs = (P(("img", "txt"), None), P(("txt", "img"), None))
    out_specs = (P(("img", "txt"), None), P(("txt", "img"), None), P(("img", "txt")))
    return jax.shard_map(
        on_device, mesh=mesh, in_specs=in_specs, out_specs=out_specs, check_vma=False
    )
```

```python
import functools

import jax
import jax.numpy as jnp
from jax import lax
from jax.experimental import pallas as pl
from jax.experimental.pallas import tpu as pltpu
from jax.sharding import PartitionSpec as P

MESH = pl.DeviceIdType.MESH
F32, BF16 = jnp.float32, jnp.bfloat16
LOG2E, LN2 = 1.4426950408889634, 0.6931471805599453
logit_scale = 100.0
logit_bias = -12.0
D = 1152
X, Y, Z, C = range(4)
SIZES = (4, 4, 8, 2)
SIGNS = (1, -1)

IMG_AT = [(0, 0), (1, 0), (3, 0), (0, 1), (0, 3), (1, 1), (1, 3), (3, 1), (3, 3), (2, 0), (0, 2), (2, 1), (2, 3), (1, 2), (3, 2), (2, 2)]
REP_AT = [0, 1, 7, 2, 6, 3, 5, 4]
IMG_POS = {o: n for n, o in enumerate(IMG_AT)}
REP_POS = {o: n for n, o in enumerate(REP_AT)}
JS = (2, 1, 3, 0)
TILES = [(0, 5, 0, 3), (5, 5, 0, 3), (0, 10, 3, 2), (10, 3, 0, 5), (0, 13, 5, 2), (13, 3, 0, 5), (13, 3, 5, 3), (0, 13, 7, 1)]


def shift(o, axis, by):
    o = list(o)
    o[axis] = (o[axis] + by) % 4
    return tuple(o)


def at(h, j, dq):
    return (j, dq % 4) if h == 0 else (dq % 4, j)


def z_chunks(s):
    return (0, 1, 2, 3) if s == 1 else (2, 3, 0, 1)


def plan():
    steps = []

    def add(name, axis, step, rows, needs):
        steps.append((name, axis, step, rows, list(dict.fromkeys(needs))))
        return [name]

    img = {((0, 0), h, u): [] for h in (0, 1) for u in (0, 1)}
    for h in (0, 1):
        p, q = h, 1 - h
        for u in (0, 1):
            for s in SIGNS:
                img[shift((0, 0), p, -s), h, u] = add(("g1", h, s, u), p, s, 16, [])
        for n, s in enumerate(SIGNS):
            src = shift((0, 0), p, -s)
            img[shift(src, p, -s), h, n] = add(("g2", h, s), p, s, 16, img[src, h, n])
        for j in (0, 1, 3, 2):
            line = shift((0, 0), p, j)
            for u in (0, 1):
                for s in SIGNS:
                    img[shift(line, q, -s), h, u] = add(("g3", h, s, j, u), q, s, 16, img[line, h, u])
            for n, s in enumerate(SIGNS):
                src = shift(line, q, -s)
                img[shift(src, q, -s), h, n] = add(("g4", h, s, j), q, s, 16, img[src, h, n])
    rep = {(0, c): [] for c in range(4)}
    for s in SIGNS:
        for d in (1, 2, 3, 4):
            for c in z_chunks(s)[: 4 if d < 4 else 2]:
                rep[-s * d % 8, c] = add(("z", d, s, c), Z, s, 16, rep[-s * (d - 1) % 8, c])
    whole = {}
    for o in REP_AT:
        mine = [n for c in range(4) for n in rep[o, c]]
        whole[o] = mine + add(("cg", o), C, 1, 64, mine)
    cover = {}
    for i, ni, r, nr in TILES:
        needs = [n for k in range(i, i + ni) for h in (0, 1) for u in (0, 1) for n in img[IMG_AT[k], h, u]]
        needs += [n for k in range(r, r + nr) for n in whole[REP_AT[k]]]
        add(("tile", i, ni, r, nr), None, 0, ni * nr, needs)
        for k in range(i, i + ni):
            for m in range(r, r + nr):
                cover[k, m] = ("tile", i, ni, r, nr)
    img_tiles = lambda blocks: [cover[IMG_POS[o], m] for o in blocks for m in range(8)]
    rep_tiles = lambda blocks: [cover[k, REP_POS[o]] for o in blocks for k in range(16)]
    add("ig2", None, 0, 256, img_tiles([at(h, j, 2) for h in (0, 1) for j in JS]))
    for h in (0, 1):
        add(("ig1", h), None, 0, 256, img_tiles([at(h, j, s) for s in SIGNS for j in JS]))
    add("ig0", None, 0, 256, img_tiles([at(h, j, 0) for h in (0, 1) for j in JS]))
    for d in (4, 3, 2, 1):
        add(("rg", d), None, 0, 256, rep_tiles([d, 0] if d == 4 else [d, 8 - d]))
    for d in (4, 3, 2, 1, 0):
        for o in (d, 8 - d) if d in (1, 2, 3) else (d,):
            add(("cr", o), C, 1, 64, [("rg", d or 4)])
    for s in SIGNS:
        order = z_chunks(s)
        for c in order[:2]:
            add(("rz", 4, s, c), Z, s, 16, [("cr", 4)])
        for d in (3, 2, 1):
            for c in order[2:] + order[:2]:
                before = [] if d == 3 and c in order[2:] else [("rz", d + 1, s, c)]
                add(("rz", d, s, c), Z, s, 16, [("cr", s * d % 8)] + before)
    for h in (0, 1):
        p, q = h, 1 - h
        for s in SIGNS:
            for j in JS:
                add(("r1", h, s, 0, j), q, s, 16, ["ig2"])
                add(("r1", h, s, 1, j), q, s, 16, [("ig1", h)])
                add(("r1", h, s, 2, j), q, s, 16, [("ig1", h), ("r1", h, s, 0, j)])
        for n, s in enumerate(SIGNS):
            line = lambda j, u: ["ig0", ("r1", h, SIGNS[u], 2, j), ("r1", h, SIGNS[1 - u], 1, j)]
            add(("r2", h, s, 0), p, s, 16, line(2, n))
            add(("r2", h, s, 1), p, s, 16, line(s % 4, 1 - n))
            add(("r2", h, s, 2), p, s, 16, line(s % 4, n) + [("r2", h, s, 0)])
    add("loss", None, 0, 0, list(cover.values()))
    for d in (1, 2, 3):
        add(("lx", d), X, d, 2, ["loss"])
    for d in (1, 2, 3):
        add(("ly", d), Y, d, 2, [("lx", e) for e in (1, 2, 3)])
    add("out_rep", None, 0, 0, [("cr", 0)] + [("rz", 1, s, c) for s in SIGNS for c in range(4)])
    lines = [("r1", h, s, k, 0) for h in (0, 1) for s in SIGNS for k in (1, 2)]
    add("out_img", None, 0, 0, ["ig0"] + lines + [("r2", h, s, k) for h in (0, 1) for s in SIGNS for k in (1, 2)])
    add("out_loss", None, 0, 0, [("ly", d) for d in (1, 2, 3)])
    return steps


SENDS = ("g1", "g2", "g3", "g4", "z", "cg", "cr", "rz", "r1", "r2", "lx", "ly")

ORDER = [
    0, 61, 60, 74, 75, 3, 39, 30, 38, 31, 6, 33, 88, 2, 62, 77, 1, 32, 7, 36, 63, 76, 37, 8, 9, 4, 65, 18, 78, 19, 5,
    48, 43, 34, 15, 64, 79, 42, 45, 14, 35, 66, 81, 44, 51, 12, 21, 67, 90, 80, 89, 50, 41, 20, 11, 69, 82, 40, 49,
    24, 27, 96, 68, 83, 54, 13, 22, 55, 70, 85, 52, 57, 26, 25, 92, 71, 84, 91, 46, 53, 10, 17, 73, 86, 56, 47, 16,
    23, 28, 29, 72, 87, 58, 98, 59, 94, 93, 97, 99, 95, 100, 101, 103, 102, 108, 119, 112, 104, 154, 166, 148, 190,
    178, 163, 184, 193, 109, 114, 120, 135, 134, 113, 121, 151, 157, 187, 160, 196, 169, 181, 199, 105, 164, 158, 136,
    155, 137, 122, 161, 123, 106, 192, 180, 179, 200, 165, 149, 139, 150, 124, 110, 116, 115, 162, 191, 182, 197, 153,
    186, 168, 138, 125, 152, 111, 198, 167, 183, 185, 194, 140, 127, 126, 156, 117, 118, 159, 171, 143, 208, 209, 195,
    128, 189, 210, 211, 170, 141, 107, 202, 172, 205, 142, 129, 175, 201, 206, 173, 144, 188, 131, 176, 147, 130, 212,
    213, 214, 203, 145, 132, 204, 207, 174, 146, 133, 177, 217, 216, 215,
]


def my_coords():
    i, t = lax.axis_index("img"), lax.axis_index("txt")
    x, z_hi = lax.rem(t, 4), lax.div(t, 4)
    y, z_lo, c = lax.div(i, 4), lax.rem(lax.div(i, 2), 2), lax.rem(i, 2)
    return (x, y, z_hi * 2 + z_lo, c)


def device_at(co, axis, step):
    co = list(co)
    co[axis] = lax.rem(co[axis] + step + SIZES[axis], SIZES[axis])
    x, y, z, c = co
    return (y * 4 + lax.rem(z, 2) * 2 + c, lax.div(z, 2) * 4 + x)


def unit_rows(ref):
    wide = ref[...].astype(F32)
    inverse = lax.rsqrt(jnp.sum(wide * wide, axis=1, keepdims=True) + 1e-06)
    return wide * inverse, inverse


def project_back(grads, unit_wide, inverse):
    return inverse * (grads - unit_wide * jnp.sum(unit_wide * grads, axis=1, keepdims=True))


def kernel(
    img_ref, rep_ref, gimg_ref, grep_ref, loss_ref,
    own_img, own_rep, ibuf, rbuf, slopes, above, below, gr, ga1, gy,
    st_c, ld_c, st_z, ld_z, st1, ld1, st2, ld2, lb_s, lb_l, lw_s, lw_l,
    ssem, rsem, own_sem,
):
    me = my_coords()
    peers = [(X, 1), (X, -1), (X, 2), (Y, 1), (Y, -1), (Y, 2), (Z, 1), (Z, -1), (C, 1)]
    barrier = pltpu.get_barrier_semaphore()
    for axis, step in peers:
        pl.semaphore_signal(barrier, inc=1, device_id=device_at(me, axis, step), device_id_type=MESH)
    loads = [
        pltpu.make_async_copy(img_ref, own_img, own_sem.at[0]),
        pltpu.make_async_copy(rep_ref, own_rep, own_sem.at[1]),
    ]
    for load in loads:
        load.start()
    above[...] = jnp.zeros_like(above)
    below[...] = jnp.zeros_like(below)
    lb_s[...] = jnp.zeros_like(lb_s)
    for load in loads:
        load.wait()
    ibuf[0] = unit_rows(own_img)[0].astype(BF16)
    rbuf[0, 0] = unit_rows(own_rep)[0].astype(BF16)
    pl.semaphore_wait(barrier, len(peers))

    def quarter(n, count=1):
        return pl.ds(n * 16, count * 16)

    matched = jnp.logical_and(me[Y] == lax.div(me[Z], 2), me[X] == lax.rem(me[Z], 2) * 2 + me[C])
    aside = jnp.where(matched, 0, 1 << 20)
    row_in = lax.broadcasted_iota(jnp.int32, (64, 1), 0)
    col_in = lax.broadcasted_iota(jnp.int32, (1, 128), 1)

    def tile(i, ni, r, nr):
        m = ni * 64
        lhs = ibuf[i : i + ni].reshape(m, D)
        rhs = rbuf[r : r + nr].reshape(nr * 128, D)
        dots = lax.dot_general(lhs, rhs, (((1,), (1,)), ((), ())), preferred_element_type=F32)
        row_ids = []
        for dx, dy in IMG_AT[i : i + ni]:
            block = lax.rem(me[Y] + dy, 4) * 4 + lax.rem(me[X] + dx, 4)
            row_ids.append(block * 64 + aside + row_in)
        row_ids = jnp.concatenate(row_ids, axis=0)
        high = above[i : i + ni].reshape(m, 128)
        low = below[i : i + ni].reshape(m, 128)
        for k in range(nr):
            bz = lax.rem(me[Z] + REP_AT[r + k], 8) * 2
            mine, other = (bz + me[C]) * 64, (bz + 1 - me[C]) * 64
            col_ids = jnp.where(col_in < 64, mine + col_in, other + col_in - 64)
            sign = jnp.where(row_ids == col_ids, -1.0, 1.0)
            bits = (dots[:, k * 128 : k * 128 + 128] * (logit_scale * LOG2E) + logit_bias * LOG2E) * sign
            e = jnp.exp2(-jnp.abs(bits))
            one_e = 1.0 + e
            inverse = 1.0 / one_e
            slope = jnp.where(bits >= 0, inverse, e * inverse) * sign
            slopes[i : i + ni, :, (r + k) * 128 : (r + k) * 128 + 128] = slope.astype(BF16).reshape(ni, 64, 128)
            high = high + jnp.maximum(bits, 0.0)
            low = low * one_e + e
        above[i : i + ni] = high.reshape(ni, 64, 128)
        below[i : i + ni] = low.reshape(ni, 64, 128)

    def img_terms(pieces):
        lhs = jnp.concatenate([slopes[IMG_POS[at(*n)], quarter(2 * n[0], 2)] for n in pieces], axis=0)
        return logit_scale * jnp.dot(lhs, rbuf[...].reshape(1024, D), preferred_element_type=F32)

    def rep_terms(offsets):
        cols = [slopes[:, :, REP_POS[o] * 128 : REP_POS[o] * 128 + 128].reshape(1024, 128) for o in offsets]
        out = logit_scale * lax.dot_general(
            jnp.concatenate(cols, axis=1), ibuf[...].reshape(1024, D), (((0,), (0,)), ((), ())),
            preferred_element_type=F32,
        )
        for n, o in enumerate(offsets):
            gr[REP_POS[o]] = out[n * 128 : n * 128 + 64]
            st_c[REP_POS[o]] = out[n * 128 + 64 : n * 128 + 128].astype(BF16)

    def far_terms():
        out = img_terms([(h, j, 2) for h in (0, 1) for j in JS])
        for h in (0, 1):
            for k in range(4):
                for n in (0, 1):
                    base = (h * 4 + k) * 32 + n * 16
                    st1[h, n, 0, k] = out[base : base + 16].astype(BF16)

    def near_terms(h):
        out = img_terms([(h, j, s) for s in SIGNS for j in JS])
        for n in (0, 1):
            for k in range(4):
                base = (n * 4 + k) * 32
                quarters = [out[base : base + 16], out[base + 16 : base + 32]]
                st1[h, n, 1, k] = quarters[1 - n].astype(BF16)
                ga1[h, n, k] = quarters[n]

    def line_terms():
        out = img_terms([(h, j, 0) for h in (0, 1) for j in JS])
        for h in (0, 1):
            for k in range(4):
                gy[h, k] = out[(h * 4 + k) * 32 : (h * 4 + k) * 32 + 32]

    def line_sum(h, j, u):
        k = JS.index(j)
        total = gy[h, k, quarter(u)] + ld1[h, u, 2, k].astype(F32)
        return total + ld1[h, 1 - u, 1, k].astype(F32)

    def paired(o, c):
        return gr[REP_POS[o % 8], quarter(c)] + ld_c[REP_POS[o % 8], quarter(c)].astype(F32)

    def losses():
        for k in range(8):
            wide = above[2 * k : 2 * k + 2] * LN2 + jnp.log1p(below[2 * k : 2 * k + 2])
            line = jnp.sum(wide.reshape(128, 128).T, axis=0, keepdims=True)
            for n in (0, 1):
                dx, dy = IMG_AT[2 * k + n]
                lb_s[dx, dy : dy + 1, :] = line if n == 0 else pltpu.roll(line, 64, 1)

    def x_losses():
        lw_s[...] = lb_s[0] + lb_l[1] + lb_l[2] + lb_l[3]

    def out_rep():
        parts = [paired(0, c) + ld_z[0, 0, c].astype(F32) + ld_z[1, 0, c].astype(F32) for c in range(4)]
        unit, inverse = unit_rows(own_rep)
        grep_ref[...] = project_back(jnp.concatenate(parts, axis=0), unit, inverse)

    def out_img():
        parts = [
            line_sum(h, 0, u) + ld2[h, u, 2].astype(F32) + ld2[h, 1 - u, 1].astype(F32)
            for h in (0, 1)
            for u in (0, 1)
        ]
        unit, inverse = unit_rows(own_img)
        gimg_ref[...] = project_back(jnp.concatenate(parts, axis=0), unit, inverse)

    def out_loss():
        loss = lw_s[0:1, :]
        for d in (1, 2, 3):
            loss = loss + lw_l[d, d : d + 1, :]
        loss_ref[...] = jnp.broadcast_to(loss, loss_ref.shape)

    compute = {
        "tile": tile, "ig2": far_terms, "ig1": near_terms, "ig0": line_terms,
        "rg": lambda d: rep_terms([4, 0] if d == 4 else [d, 8 - d]),
        "loss": losses, "out_rep": out_rep, "out_img": out_img, "out_loss": out_loss,
    }

    def img_ends(o, part, axis, s):
        return ibuf.at[IMG_POS[o], part], ibuf.at[IMG_POS[shift(o, axis, -s)], part]

    def ends(name):
        kind, a = name[0], name[1:]
        if kind == "g1":
            h, s, u = a
            return img_ends((0, 0), quarter(2 * h + u), h, s)
        if kind == "g2":
            h, s = a
            return img_ends(shift((0, 0), h, -s), quarter(2 * h + SIGNS.index(s)), h, s)
        if kind == "g3":
            h, s, j, u = a
            return img_ends(at(h, j, 0), quarter(2 * h + u), 1 - h, s)
        if kind == "g4":
            h, s, j = a
            return img_ends(at(h, j, -s), quarter(2 * h + SIGNS.index(s)), 1 - h, s)
        if kind == "z":
            d, s, c = a
            return (
                rbuf.at[REP_POS[-s * (d - 1) % 8], 0, quarter(c)],
                rbuf.at[REP_POS[-s * d % 8], 0, quarter(c)],
            )
        if kind == "cg":
            return rbuf.at[REP_POS[a[0]], 0], rbuf.at[REP_POS[a[0]], 1]
        if kind == "cr":
            return st_c.at[REP_POS[a[0]]], ld_c.at[REP_POS[a[0]]]
        if kind == "rz":
            d, s, c = a
            return st_z.at[SIGNS.index(s), d - 1, c], ld_z.at[SIGNS.index(s), d - 1, c]
        if kind == "r1":
            h, s, slot, j = a
            where = (h, SIGNS.index(s), slot, JS.index(j))
            return st1.at[where], ld1.at[where]
        if kind == "r2":
            h, s, slot = a
            return st2.at[h, SIGNS.index(s), slot], ld2.at[h, SIGNS.index(s), slot]
        if kind == "lx":
            return lb_s.at[a[0]], lb_l.at[a[0]]
        return lw_s, lw_l.at[a[0]]

    def prepare(name):
        kind, a = name[0], name[1:]
        if kind == "rz":
            d, s, c = a
            n = SIGNS.index(s)
            term = paired(s * d, c)
            if d < 3 or (d == 3 and c in z_chunks(s)[:2]):
                term = term + ld_z[n, d, c].astype(F32)
            st_z[n, d - 1, c] = term.astype(BF16)
        if kind == "r1" and a[2] == 2:
            h, s, _, j = a
            n, k = SIGNS.index(s), JS.index(j)
            st1[h, n, 2, k] = (ga1[h, n, k] + ld1[h, n, 0, k].astype(F32)).astype(BF16)
        if kind == "r2":
            h, s, slot = a
            n = SIGNS.index(s)
            term = line_sum(h, 2 if slot == 0 else s % 4, 1 - n if slot == 1 else n)
            if slot == 2:
                term = term + ld2[h, n, 0].astype(F32)
            st2[h, n, slot] = term.astype(BF16)
        if name == ("ly", 1):
            x_losses()

    steps = plan()
    copies = {}
    for name, axis, step, _, _ in steps:
        if axis is not None:
            k = len(copies)
            src, dst = ends(name)
            copies[name] = pltpu.make_async_remote_copy(
                src, dst, ssem.at[SENDS.index(name[0])], rsem.at[k], device_id=device_at(me, axis, step), device_id_type=MESH
            )
    arrived = set()
    for n in ORDER:
        name, axis, _, _, needs = steps[n]
        for need in needs:
            if need in copies and need not in arrived:
                copies[need].wait_recv()
                arrived.add(need)
        if axis is None:
            args = () if isinstance(name, str) else name[1:]
            compute[name if isinstance(name, str) else name[0]](*args)
        else:
            prepare(name)
            copies[name].start()
    sent = {
        "g1": ibuf.at[pl.ds(0, 2)], "g2": ibuf.at[pl.ds(0, 1)], "g3": ibuf.at[pl.ds(0, 8)], "g4": ibuf.at[pl.ds(0, 4)],
        "z": rbuf.at[pl.ds(0, 7), 0], "cg": rbuf.at[:, 0], "cr": st_c, "rz": rbuf.at[pl.ds(0, 7), 0],
        "r1": st1, "r2": st2, "lx": lb_s.at[pl.ds(1, 3)], "ly": lw_l.at[pl.ds(1, 3)],
    }
    for n, kind in enumerate(SENDS):
        pltpu.make_async_remote_copy(
            sent[kind], sent[kind], ssem.at[n], rsem.at[0], device_id=device_at(me, C, 1), device_id_type=MESH
        ).wait_send()


def finish(gimg, grep, loss, out_img, out_rep, out_loss, sem):
    stores = [pltpu.make_async_copy(gimg, out_img, sem.at[0]), pltpu.make_async_copy(grep, out_rep, sem.at[1])]
    for store in stores:
        store.start()
    out_loss[...] = loss[0, :64]
    for store in stores:
        store.wait()


COPIES = sum(step[1] is not None for step in plan())


def on_device(image_emb, report_emb):
    vmem = pl.BlockSpec(memory_space=pltpu.VMEM)
    hbm = pl.BlockSpec(memory_space=pl.ANY)
    sums = (
        jax.ShapeDtypeStruct((64, D), F32),
        jax.ShapeDtypeStruct((64, D), F32),
        jax.ShapeDtypeStruct((8, 128), F32),
    )
    gimg, grep, loss = pl.pallas_call(
        kernel,
        out_shape=(pltpu.VMEM((64, D), F32), pltpu.VMEM((64, D), F32), pltpu.VMEM((8, 128), F32)),
        in_specs=[pl.BlockSpec(memory_space=pltpu.HBM)] * 2,
        out_specs=(vmem, vmem, vmem),
        scratch_shapes=[
            pltpu.VMEM((64, D), BF16),
            pltpu.VMEM((64, D), BF16),
            pltpu.VMEM((16, 64, D), BF16),
            pltpu.VMEM((8, 2, 64, D), BF16),
            pltpu.VMEM((16, 64, 1024), BF16),
            pltpu.VMEM((16, 64, 128), F32),
            pltpu.VMEM((16, 64, 128), F32),
            pltpu.VMEM((8, 64, D), F32),
            pltpu.VMEM((2, 2, 4, 16, D), F32),
            pltpu.VMEM((2, 4, 32, D), F32),
            pltpu.VMEM((8, 64, D), BF16),
            pltpu.VMEM((8, 64, D), BF16),
            pltpu.VMEM((2, 4, 4, 16, D), BF16),
            pltpu.VMEM((2, 4, 4, 16, D), BF16),
            pltpu.VMEM((2, 2, 3, 4, 16, D), BF16),
            pltpu.VMEM((2, 2, 3, 4, 16, D), BF16),
            pltpu.VMEM((2, 2, 3, 16, D), BF16),
            pltpu.VMEM((2, 2, 3, 16, D), BF16),
            pltpu.VMEM((4, 8, 128), F32),
            pltpu.VMEM((4, 8, 128), F32),
            pltpu.VMEM((8, 128), F32),
            pltpu.VMEM((4, 8, 128), F32),
            pltpu.SemaphoreType.DMA((len(SENDS),)),
            pltpu.SemaphoreType.DMA((COPIES,)),
            pltpu.SemaphoreType.DMA((2,)),
        ],
        compiler_params=pltpu.CompilerParams(
            collective_id=0, has_side_effects=True, vmem_limit_bytes=40 * 2**20
        ),
        cost_estimate=pl.CostEstimate(
            flops=3 * 2 * 1024 * 1024 * D, bytes_accessed=900000, transcendentals=3 * 1024 * 1024
        ),
    )(pltpu.with_memory_space_constraint(image_emb, pltpu.HBM), pltpu.with_memory_space_constraint(report_emb, pltpu.HBM))
    return pl.pallas_call(
        finish,
        out_shape=sums[:2] + (jax.ShapeDtypeStruct((64,), F32),),
        in_specs=[vmem, vmem, vmem],
        out_specs=(hbm, hbm, vmem),
        scratch_shapes=[pltpu.SemaphoreType.DMA((2,))],
        compiler_params=pltpu.CompilerParams(vmem_limit_bytes=8 * 2**20),
    )(gimg, grep, loss)


def solution(mesh):
    in_specs = (P(("img", "txt"), None), P(("txt", "img"), None))
    out_specs = (P(("img", "txt"), None), P(("txt", "img"), None), P(("img", "txt")))
    return jax.shard_map(
        on_device, mesh=mesh, in_specs=in_specs, out_specs=out_specs, check_vma=False
    )
```

```python
import functools

import jax
import jax.numpy as jnp
from jax import lax
from jax.experimental import pallas as pl
from jax.experimental.pallas import tpu as pltpu
from jax.sharding import PartitionSpec as P

MESH = pl.DeviceIdType.MESH
F32, BF16 = jnp.float32, jnp.bfloat16
LOG2E, LN2 = 1.4426950408889634, 0.6931471805599453
logit_scale = 100.0
logit_bias = -12.0
D = 1152
X, Y, Z, C = range(4)
SIZES = (4, 4, 8, 2)
SIGNS = (1, -1)

IMG_AT = [(0, 0), (1, 0), (3, 0), (0, 1), (0, 3), (1, 1), (1, 3), (3, 1), (3, 3), (2, 0), (0, 2), (2, 1), (2, 3), (1, 2), (3, 2), (2, 2)]
REP_AT = [0, 1, 7, 2, 6, 3, 5, 4]
IMG_POS = {o: n for n, o in enumerate(IMG_AT)}
REP_POS = {o: n for n, o in enumerate(REP_AT)}
JS = (2, 1, 3, 0)
TILES = [(0, 5, 0, 3), (5, 5, 0, 3), (0, 10, 3, 2), (10, 3, 0, 5), (0, 13, 5, 2), (13, 3, 0, 5), (13, 3, 5, 3), (0, 13, 7, 1)]


def shift(o, axis, by):
    o = list(o)
    o[axis] = (o[axis] + by) % 4
    return tuple(o)


def at(h, j, dq):
    return (j, dq % 4) if h == 0 else (dq % 4, j)


def z_chunks(s):
    return (0, 1, 2, 3) if s == 1 else (2, 3, 0, 1)


def plan():
    steps = []

    def add(name, axis, step, rows, needs):
        steps.append((name, axis, step, rows, list(dict.fromkeys(needs))))
        return [name]

    img = {((0, 0), h, u): [] for h in (0, 1) for u in (0, 1)}
    for h in (0, 1):
        p, q = h, 1 - h
        for u in (0, 1):
            for s in SIGNS:
                img[shift((0, 0), p, -s), h, u] = add(("g1", h, s, u), p, s, 16, [])
        for n, s in enumerate(SIGNS):
            src = shift((0, 0), p, -s)
            img[shift(src, p, -s), h, n] = add(("g2", h, s), p, s, 16, img[src, h, n])
        for j in (0, 1, 3, 2):
            line = shift((0, 0), p, j)
            for u in (0, 1):
                for s in SIGNS:
                    img[shift(line, q, -s), h, u] = add(("g3", h, s, j, u), q, s, 16, img[line, h, u])
            for n, s in enumerate(SIGNS):
                src = shift(line, q, -s)
                img[shift(src, q, -s), h, n] = add(("g4", h, s, j), q, s, 16, img[src, h, n])
    rep = {(0, c): [] for c in range(4)}
    for s in SIGNS:
        for d in (1, 2, 3, 4):
            for c in z_chunks(s)[: 4 if d < 4 else 2]:
                rep[-s * d % 8, c] = add(("z", d, s, c), Z, s, 16, rep[-s * (d - 1) % 8, c])
    whole = {}
    for o in REP_AT:
        mine = [n for c in range(4) for n in rep[o, c]]
        whole[o] = mine + add(("cg", o), C, 1, 64, mine)
    cover = {}
    for i, ni, r, nr in TILES:
        needs = [n for k in range(i, i + ni) for h in (0, 1) for u in (0, 1) for n in img[IMG_AT[k], h, u]]
        needs += [n for k in range(r, r + nr) for n in whole[REP_AT[k]]]
        add(("tile", i, ni, r, nr), None, 0, ni * nr, needs)
        for k in range(i, i + ni):
            for m in range(r, r + nr):
                cover[k, m] = ("tile", i, ni, r, nr)
    img_tiles = lambda blocks: [cover[IMG_POS[o], m] for o in blocks for m in range(8)]
    rep_tiles = lambda blocks: [cover[k, REP_POS[o]] for o in blocks for k in range(16)]
    add("ig2", None, 0, 256, img_tiles([at(h, j, 2) for h in (0, 1) for j in JS]))
    for h in (0, 1):
        add(("ig1", h), None, 0, 256, img_tiles([at(h, j, s) for s in SIGNS for j in JS]))
    add("ig0", None, 0, 256, img_tiles([at(h, j, 0) for h in (0, 1) for j in JS]))
    for d in (4, 3, 2, 1, 0):
        add(("rg", d), None, 0, 256, rep_tiles([d] if d in (0, 4) else [d, 8 - d]))
    for d in (4, 3, 2, 1, 0):
        for o in (d, 8 - d) if d in (1, 2, 3) else (d,):
            add(("cr", o), C, 1, 64, [("rg", d)])
    for s in SIGNS:
        order = z_chunks(s)
        for c in order[:2]:
            add(("rz", 4, s, c), Z, s, 16, [("cr", 4)])
        for d in (3, 2, 1):
            for c in order[2:] + order[:2]:
                before = [] if d == 3 and c in order[2:] else [("rz", d + 1, s, c)]
                add(("rz", d, s, c), Z, s, 16, [("cr", s * d % 8)] + before)
    for h in (0, 1):
        p, q = h, 1 - h
        for s in SIGNS:
            for j in JS:
                add(("r1", h, s, 0, j), q, s, 16, ["ig2"])
                add(("r1", h, s, 1, j), q, s, 16, [("ig1", h)])
                add(("r1", h, s, 2, j), q, s, 16, [("ig1", h), ("r1", h, s, 0, j)])
        for n, s in enumerate(SIGNS):
            line = lambda j, u: ["ig0", ("r1", h, SIGNS[u], 2, j), ("r1", h, SIGNS[1 - u], 1, j)]
            add(("r2", h, s, 0), p, s, 16, line(2, n))
            add(("r2", h, s, 1), p, s, 16, line(s % 4, 1 - n))
            add(("r2", h, s, 2), p, s, 16, line(s % 4, n) + [("r2", h, s, 0)])
    add("loss", None, 0, 0, list(cover.values()))
    for d in (1, 2, 3):
        add(("lx", d), X, d, 2, ["loss"])
    for d in (1, 2, 3):
        add(("ly", d), Y, d, 2, [("lx", e) for e in (1, 2, 3)])
    add("out_rep", None, 0, 0, [("cr", 0)] + [("rz", 1, s, c) for s in SIGNS for c in range(4)])
    lines = [("r1", h, s, k, 0) for h in (0, 1) for s in SIGNS for k in (1, 2)]
    add("out_img", None, 0, 0, ["ig0"] + lines + [("r2", h, s, k) for h in (0, 1) for s in SIGNS for k in (1, 2)])
    add("out_loss", None, 0, 0, [("ly", d) for d in (1, 2, 3)])
    return steps


SENDS = ("g1", "g2", "g3", "g4", "z", "cg", "cr", "rz", "r1", "r2", "lx", "ly")

ORDER = [
    60, 61, 74, 75, 0, 3, 30, 33, 31, 32, 1, 2, 88, 62, 76, 36, 39, 6, 9, 63, 77, 38, 37, 8, 7, 64, 78, 4, 5, 34, 35,
    45, 48, 15, 18, 44, 65, 14, 79, 19, 49, 42, 66, 51, 80, 12, 21, 40, 67, 10, 81, 11, 41, 89, 90, 50, 43, 20, 13,
    68, 82, 54, 57, 24, 27, 96, 69, 83, 52, 47, 26, 25, 70, 84, 56, 55, 22, 17, 71, 92, 85, 91, 46, 53, 16, 23, 72,
    86, 98, 73, 87, 58, 28, 29, 59, 97, 94, 93, 99, 100, 95, 101, 110, 116, 117, 103, 102, 108, 113, 104, 149, 161,
    179, 191, 152, 164, 182, 194, 121, 122, 135, 136, 109, 114, 115, 155, 167, 185, 197, 158, 170, 188, 200, 105, 123,
    124, 150, 162, 106, 137, 138, 180, 151, 163, 181, 192, 193, 153, 165, 107, 125, 126, 139, 154, 140, 166, 183, 184,
    195, 209, 210, 211, 212, 156, 168, 196, 111, 127, 157, 169, 186, 198, 118, 187, 119, 112, 128, 141, 199, 159, 171,
    189, 120, 201, 160, 172, 142, 173, 176, 129, 203, 206, 143, 190, 202, 130, 213, 214, 215, 144, 174, 204, 131, 177,
    132, 145, 207, 146, 133, 147, 175, 134, 178, 205, 208, 148, 218, 217, 216,
]


def group_of(name):
    last = (name[0] == "r2" and name[3] > 0) or (name[0] == "rz" and name[1] == 1) or name[0] in ("lx", "ly")
    return name[0] if last else name


def my_coords():
    i, t = lax.axis_index("img"), lax.axis_index("txt")
    x, z_hi = lax.rem(t, 4), lax.div(t, 4)
    y, z_lo, c = lax.div(i, 4), lax.rem(lax.div(i, 2), 2), lax.rem(i, 2)
    return (x, y, z_hi * 2 + z_lo, c)


def device_at(co, axis, step):
    co = list(co)
    co[axis] = lax.rem(co[axis] + step + SIZES[axis], SIZES[axis])
    x, y, z, c = co
    return (y * 4 + lax.rem(z, 2) * 2 + c, lax.div(z, 2) * 4 + x)


def unit_rows(ref):
    wide = ref[...].astype(F32)
    inverse = lax.rsqrt(jnp.sum(wide * wide, axis=1, keepdims=True) + 1e-06)
    return wide * inverse, inverse


def project_back(grads, unit_wide, inverse):
    return inverse * (grads - unit_wide * jnp.sum(unit_wide * grads, axis=1, keepdims=True))


def kernel(
    img_ref, rep_ref, gimg_ref, grep_ref, loss_ref,
    own_img, own_rep, ibuf, rbuf, slopes, above, below, gr, ga1, gy,
    st_c, ld_c, st_z, ld_z, st1, ld1, st2, ld2, lb_s, lb_l, lw_s, lw_l,
    ssem, rsem, own_sem,
):
    me = my_coords()
    peers = [(X, 1), (X, -1), (X, 2), (Y, 1), (Y, -1), (Y, 2), (Z, 1), (Z, -1), (C, 1)]
    barrier = pltpu.get_barrier_semaphore()
    for axis, step in peers:
        pl.semaphore_signal(barrier, inc=1, device_id=device_at(me, axis, step), device_id_type=MESH)
    loads = [
        pltpu.make_async_copy(img_ref, own_img, own_sem.at[0]),
        pltpu.make_async_copy(rep_ref, own_rep, own_sem.at[1]),
    ]
    for load in loads:
        load.start()
    above[...] = jnp.zeros_like(above)
    below[...] = jnp.zeros_like(below)
    lb_s[...] = jnp.zeros_like(lb_s)
    for load in loads:
        load.wait()
    ibuf[0] = unit_rows(own_img)[0].astype(BF16)
    rbuf[0, 0] = unit_rows(own_rep)[0].astype(BF16)
    pl.semaphore_wait(barrier, len(peers))

    def quarter(n, count=1):
        return pl.ds(n * 16, count * 16)

    matched = jnp.logical_and(me[Y] == lax.div(me[Z], 2), me[X] == lax.rem(me[Z], 2) * 2 + me[C])
    aside = jnp.where(matched, 0, 1 << 20)
    row_in = lax.broadcasted_iota(jnp.int32, (64, 1), 0)
    col_in = lax.broadcasted_iota(jnp.int32, (1, 128), 1)

    def tile(i, ni, r, nr):
        m = ni * 64
        lhs = ibuf[i : i + ni].reshape(m, D)
        rhs = rbuf[r : r + nr].reshape(nr * 128, D)
        dots = lax.dot_general(lhs, rhs, (((1,), (1,)), ((), ())), preferred_element_type=F32)
        row_ids = []
        for dx, dy in IMG_AT[i : i + ni]:
            block = lax.rem(me[Y] + dy, 4) * 4 + lax.rem(me[X] + dx, 4)
            row_ids.append(block * 64 + aside + row_in)
        row_ids = jnp.concatenate(row_ids, axis=0)
        high = above[i : i + ni].reshape(m, 128)
        low = below[i : i + ni].reshape(m, 128)
        for k in range(nr):
            bz = lax.rem(me[Z] + REP_AT[r + k], 8) * 2
            mine, other = (bz + me[C]) * 64, (bz + 1 - me[C]) * 64
            col_ids = jnp.where(col_in < 64, mine + col_in, other + col_in - 64)
            sign = jnp.where(row_ids == col_ids, -1.0, 1.0)
            bits = (dots[:, k * 128 : k * 128 + 128] * (logit_scale * LOG2E) + logit_bias * LOG2E) * sign
            e = jnp.exp2(-jnp.abs(bits))
            one_e = 1.0 + e
            inverse = 1.0 / one_e
            slope = jnp.where(bits >= 0, inverse, e * inverse) * sign
            slopes[i : i + ni, :, (r + k) * 128 : (r + k) * 128 + 128] = slope.astype(BF16).reshape(ni, 64, 128)
            high = high + jnp.maximum(bits, 0.0)
            low = low * one_e + e
        above[i : i + ni] = high.reshape(ni, 64, 128)
        below[i : i + ni] = low.reshape(ni, 64, 128)

    def img_terms(pieces):
        lhs = jnp.concatenate([slopes[IMG_POS[at(*n)], quarter(2 * n[0], 2)] for n in pieces], axis=0)
        return logit_scale * jnp.dot(lhs, rbuf[...].reshape(1024, D), preferred_element_type=F32)

    def rep_terms(offsets):
        cols = [slopes[:, :, REP_POS[o] * 128 : REP_POS[o] * 128 + 128].reshape(1024, 128) for o in offsets]
        out = logit_scale * lax.dot_general(
            jnp.concatenate(cols, axis=1) if len(cols) > 1 else cols[0], ibuf[...].reshape(1024, D), (((0,), (0,)), ((), ())),
            preferred_element_type=F32,
        )
        for n, o in enumerate(offsets):
            gr[REP_POS[o]] = out[n * 128 : n * 128 + 64]
            st_c[REP_POS[o]] = out[n * 128 + 64 : n * 128 + 128].astype(BF16)

    def far_terms():
        out = img_terms([(h, j, 2) for h in (0, 1) for j in JS])
        for h in (0, 1):
            for k in range(4):
                for n in (0, 1):
                    base = (h * 4 + k) * 32 + n * 16
                    st1[h, n, 0, k] = out[base : base + 16].astype(BF16)

    def near_terms(h):
        out = img_terms([(h, j, s) for s in SIGNS for j in JS])
        for n in (0, 1):
            for k in range(4):
                base = (n * 4 + k) * 32
                quarters = [out[base : base + 16], out[base + 16 : base + 32]]
                st1[h, n, 1, k] = quarters[1 - n].astype(BF16)
                ga1[h, n, k] = quarters[n]

    def line_terms():
        out = img_terms([(h, j, 0) for h in (0, 1) for j in JS])
        for h in (0, 1):
            for k in range(4):
                gy[h, k] = out[(h * 4 + k) * 32 : (h * 4 + k) * 32 + 32]

    def line_sum(h, j, u):
        k = JS.index(j)
        total = gy[h, k, quarter(u)] + ld1[h, u, 2, k].astype(F32)
        return total + ld1[h, 1 - u, 1, k].astype(F32)

    def paired(o, c):
        return gr[REP_POS[o % 8], quarter(c)] + ld_c[REP_POS[o % 8], quarter(c)].astype(F32)

    def losses():
        for k in range(8):
            wide = above[2 * k : 2 * k + 2] * LN2 + jnp.log1p(below[2 * k : 2 * k + 2])
            line = jnp.sum(wide.reshape(128, 128).T, axis=0, keepdims=True)
            for n in (0, 1):
                dx, dy = IMG_AT[2 * k + n]
                lb_s[dx, dy : dy + 1, :] = line if n == 0 else pltpu.roll(line, 64, 1)

    def x_losses():
        lw_s[...] = lb_s[0] + lb_l[1] + lb_l[2] + lb_l[3]

    def out_rep():
        parts = [paired(0, c) + ld_z[0, 0, c].astype(F32) + ld_z[1, 0, c].astype(F32) for c in range(4)]
        unit, inverse = unit_rows(own_rep)
        grep_ref[...] = project_back(jnp.concatenate(parts, axis=0), unit, inverse)

    def out_img():
        parts = [
            line_sum(h, 0, u) + ld2[h, u, 2].astype(F32) + ld2[h, 1 - u, 1].astype(F32)
            for h in (0, 1)
            for u in (0, 1)
        ]
        unit, inverse = unit_rows(own_img)
        gimg_ref[...] = project_back(jnp.concatenate(parts, axis=0), unit, inverse)

    def out_loss():
        loss = lw_s[0:1, :]
        for d in (1, 2, 3):
            loss = loss + lw_l[d, d : d + 1, :]
        loss_ref[...] = jnp.broadcast_to(loss, loss_ref.shape)

    compute = {
        "tile": tile, "ig2": far_terms, "ig1": near_terms, "ig0": line_terms,
        "rg": lambda d: rep_terms([d] if d in (0, 4) else [d, 8 - d]),
        "loss": losses, "out_rep": out_rep, "out_img": out_img, "out_loss": out_loss,
    }

    def img_ends(o, part, axis, s):
        return ibuf.at[IMG_POS[o], part], ibuf.at[IMG_POS[shift(o, axis, -s)], part]

    def ends(name):
        kind, a = name[0], name[1:]
        if kind == "g1":
            h, s, u = a
            return img_ends((0, 0), quarter(2 * h + u), h, s)
        if kind == "g2":
            h, s = a
            return img_ends(shift((0, 0), h, -s), quarter(2 * h + SIGNS.index(s)), h, s)
        if kind == "g3":
            h, s, j, u = a
            return img_ends(at(h, j, 0), quarter(2 * h + u), 1 - h, s)
        if kind == "g4":
            h, s, j = a
            return img_ends(at(h, j, -s), quarter(2 * h + SIGNS.index(s)), 1 - h, s)
        if kind == "z":
            d, s, c = a
            return (
                rbuf.at[REP_POS[-s * (d - 1) % 8], 0, quarter(c)],
                rbuf.at[REP_POS[-s * d % 8], 0, quarter(c)],
            )
        if kind == "cg":
            return rbuf.at[REP_POS[a[0]], 0], rbuf.at[REP_POS[a[0]], 1]
        if kind == "cr":
            return st_c.at[REP_POS[a[0]]], ld_c.at[REP_POS[a[0]]]
        if kind == "rz":
            d, s, c = a
            return st_z.at[SIGNS.index(s), d - 1, c], ld_z.at[SIGNS.index(s), d - 1, c]
        if kind == "r1":
            h, s, slot, j = a
            where = (h, SIGNS.index(s), slot, JS.index(j))
            return st1.at[where], ld1.at[where]
        if kind == "r2":
            h, s, slot = a
            return st2.at[h, SIGNS.index(s), slot], ld2.at[h, SIGNS.index(s), slot]
        if kind == "lx":
            return lb_s.at[a[0]], lb_l.at[a[0]]
        return lw_s, lw_l.at[a[0]]

    def prepare(name):
        kind, a = name[0], name[1:]
        if kind == "rz":
            d, s, c = a
            n = SIGNS.index(s)
            term = paired(s * d, c)
            if d < 3 or (d == 3 and c in z_chunks(s)[:2]):
                term = term + ld_z[n, d, c].astype(F32)
            st_z[n, d - 1, c] = term.astype(BF16)
        if kind == "r1" and a[2] == 2:
            h, s, _, j = a
            n, k = SIGNS.index(s), JS.index(j)
            st1[h, n, 2, k] = (ga1[h, n, k] + ld1[h, n, 0, k].astype(F32)).astype(BF16)
        if kind == "r2":
            h, s, slot = a
            n = SIGNS.index(s)
            term = line_sum(h, 2 if slot == 0 else s % 4, 1 - n if slot == 1 else n)
            if slot == 2:
                term = term + ld2[h, n, 0].astype(F32)
            st2[h, n, slot] = term.astype(BF16)
        if name == ("ly", 1):
            x_losses()

    steps = plan()
    copies = {}
    together = {
        "r2": ibuf.at[pl.ds(0, 2)], "rz": ibuf.at[pl.ds(0, 2)], "lx": lb_s.at[pl.ds(1, 3)], "ly": lw_l.at[pl.ds(1, 3)],
    }
    landing = {}
    for name, axis, step, _, _ in steps:
        if axis is not None:
            k = landing.setdefault(group_of(name), len(landing))
            src, dst = ends(name)
            copies[name] = pltpu.make_async_remote_copy(
                src, dst, ssem.at[SENDS.index(name[0])], rsem.at[k], device_id=device_at(me, axis, step), device_id_type=MESH
            )
    arrived = set()
    for n in ORDER:
        name, axis, _, _, needs = steps[n]
        for need in needs:
            group = group_of(need)
            if need in copies and group not in arrived:
                copy = copies[need]
                if group in together:
                    copy = pltpu.make_async_remote_copy(
                        together[group], together[group], ssem.at[0], rsem.at[landing[group]],
                        device_id=device_at(me, C, 1), device_id_type=MESH,
                    )
                copy.wait_recv()
                arrived.add(group)
        if axis is None:
            args = () if isinstance(name, str) else name[1:]
            compute[name if isinstance(name, str) else name[0]](*args)
        else:
            prepare(name)
            copies[name].start()
    sent = {
        "g1": ibuf.at[pl.ds(0, 2)], "g2": ibuf.at[pl.ds(0, 1)], "g3": ibuf.at[pl.ds(0, 8)], "g4": ibuf.at[pl.ds(0, 4)],
        "z": rbuf.at[pl.ds(0, 7), 0], "cg": rbuf.at[:, 0], "cr": st_c, "rz": rbuf.at[pl.ds(0, 7), 0],
        "r1": st1, "r2": st2, "lx": lb_s.at[pl.ds(1, 3)], "ly": lw_l.at[pl.ds(1, 3)],
    }
    for n, kind in enumerate(SENDS):
        pltpu.make_async_remote_copy(
            sent[kind], sent[kind], ssem.at[n], rsem.at[0], device_id=device_at(me, C, 1), device_id_type=MESH
        ).wait_send()


def finish(gimg, grep, loss, out_img, out_rep, out_loss, sem):
    stores = [pltpu.make_async_copy(gimg, out_img, sem.at[0]), pltpu.make_async_copy(grep, out_rep, sem.at[1])]
    for store in stores:
        store.start()
    out_loss[...] = loss[0, :64]
    for store in stores:
        store.wait()


LANDINGS = len({group_of(step[0]) for step in plan() if step[1] is not None})


def on_device(image_emb, report_emb):
    vmem = pl.BlockSpec(memory_space=pltpu.VMEM)
    hbm = pl.BlockSpec(memory_space=pl.ANY)
    sums = (
        jax.ShapeDtypeStruct((64, D), F32),
        jax.ShapeDtypeStruct((64, D), F32),
        jax.ShapeDtypeStruct((8, 128), F32),
    )
    gimg, grep, loss = pl.pallas_call(
        kernel,
        out_shape=(pltpu.VMEM((64, D), F32), pltpu.VMEM((64, D), F32), pltpu.VMEM((8, 128), F32)),
        in_specs=[pl.BlockSpec(memory_space=pltpu.HBM)] * 2,
        out_specs=(vmem, vmem, vmem),
        scratch_shapes=[
            pltpu.VMEM((64, D), BF16),
            pltpu.VMEM((64, D), BF16),
            pltpu.VMEM((16, 64, D), BF16),
            pltpu.VMEM((8, 2, 64, D), BF16),
            pltpu.VMEM((16, 64, 1024), BF16),
            pltpu.VMEM((16, 64, 128), F32),
            pltpu.VMEM((16, 64, 128), F32),
            pltpu.VMEM((8, 64, D), F32),
            pltpu.VMEM((2, 2, 4, 16, D), F32),
            pltpu.VMEM((2, 4, 32, D), F32),
            pltpu.VMEM((8, 64, D), BF16),
            pltpu.VMEM((8, 64, D), BF16),
            pltpu.VMEM((2, 4, 4, 16, D), BF16),
            pltpu.VMEM((2, 4, 4, 16, D), BF16),
            pltpu.VMEM((2, 2, 3, 4, 16, D), BF16),
            pltpu.VMEM((2, 2, 3, 4, 16, D), BF16),
            pltpu.VMEM((2, 2, 3, 16, D), BF16),
            pltpu.VMEM((2, 2, 3, 16, D), BF16),
            pltpu.VMEM((4, 8, 128), F32),
            pltpu.VMEM((4, 8, 128), F32),
            pltpu.VMEM((8, 128), F32),
            pltpu.VMEM((4, 8, 128), F32),
            pltpu.SemaphoreType.DMA((len(SENDS),)),
            pltpu.SemaphoreType.DMA((LANDINGS,)),
            pltpu.SemaphoreType.DMA((2,)),
        ],
        compiler_params=pltpu.CompilerParams(
            collective_id=0, has_side_effects=True, vmem_limit_bytes=40 * 2**20
        ),
        cost_estimate=pl.CostEstimate(
            flops=3 * 2 * 1024 * 1024 * D, bytes_accessed=900000, transcendentals=3 * 1024 * 1024
        ),
    )(pltpu.with_memory_space_constraint(image_emb, pltpu.HBM), pltpu.with_memory_space_constraint(report_emb, pltpu.HBM))
    return pl.pallas_call(
        finish,
        out_shape=sums[:2] + (jax.ShapeDtypeStruct((64,), F32),),
        in_specs=[vmem, vmem, vmem],
        out_specs=(hbm, hbm, vmem),
        scratch_shapes=[pltpu.SemaphoreType.DMA((2,))],
        compiler_params=pltpu.CompilerParams(vmem_limit_bytes=8 * 2**20),
    )(gimg, grep, loss)


def solution(mesh):
    in_specs = (P(("img", "txt"), None), P(("txt", "img"), None))
    out_specs = (P(("img", "txt"), None), P(("txt", "img"), None), P(("img", "txt")))
    return jax.shard_map(
        on_device, mesh=mesh, in_specs=in_specs, out_specs=out_specs, check_vma=False
    )
```

```python
import functools

import jax
import jax.numpy as jnp
from jax import lax
from jax.experimental import pallas as pl
from jax.experimental.pallas import tpu as pltpu
from jax.sharding import PartitionSpec as P

MESH = pl.DeviceIdType.MESH
F32, BF16 = jnp.float32, jnp.bfloat16
LOG2E, LN2 = 1.4426950408889634, 0.6931471805599453
logit_scale = 100.0
logit_bias = -12.0
D = 1152
X, Y, Z, C = range(4)
SIZES = (4, 4, 8, 2)
SIGNS = (1, -1)

IMG_AT = [(0, 0), (1, 0), (3, 0), (0, 1), (0, 3), (1, 1), (1, 3), (3, 1), (3, 3), (2, 0), (0, 2), (2, 1), (2, 3), (1, 2), (3, 2), (2, 2)]
REP_AT = [0, 1, 7, 2, 6, 3, 5, 4]
IMG_POS = {o: n for n, o in enumerate(IMG_AT)}
REP_POS = {o: n for n, o in enumerate(REP_AT)}
JS = (2, 1, 3, 0)
TILES = [(0, 5, 0, 3), (5, 5, 0, 3), (0, 10, 3, 2), (10, 3, 0, 5), (0, 13, 5, 2), (13, 3, 0, 5), (13, 3, 5, 3), (0, 13, 7, 1)]


def shift(o, axis, by):
    o = list(o)
    o[axis] = (o[axis] + by) % 4
    return tuple(o)


def at(h, j, dq):
    return (j, dq % 4) if h == 0 else (dq % 4, j)


def z_chunks(s):
    return (0, 1, 2, 3) if s == 1 else (2, 3, 0, 1)


def plan():
    steps = []

    def add(name, axis, step, rows, needs):
        steps.append((name, axis, step, rows, list(dict.fromkeys(needs))))
        return [name]

    img = {((0, 0), h, u): [] for h in (0, 1) for u in (0, 1)}
    for h in (0, 1):
        p, q = h, 1 - h
        for u in (0, 1):
            for s in SIGNS:
                img[shift((0, 0), p, -s), h, u] = add(("g1", h, s, u), p, s, 16, [])
        for n, s in enumerate(SIGNS):
            src = shift((0, 0), p, -s)
            img[shift(src, p, -s), h, n] = add(("g2", h, s), p, s, 16, img[src, h, n])
        for j in (0, 1, 3, 2):
            line = shift((0, 0), p, j)
            for u in (0, 1):
                for s in SIGNS:
                    img[shift(line, q, -s), h, u] = add(("g3", h, s, j, u), q, s, 16, img[line, h, u])
            for n, s in enumerate(SIGNS):
                src = shift(line, q, -s)
                img[shift(src, q, -s), h, n] = add(("g4", h, s, j), q, s, 16, img[src, h, n])
    rep = {(0, c): [] for c in range(4)}
    for s in SIGNS:
        for d in (1, 2, 3, 4):
            for c in z_chunks(s)[: 4 if d < 4 else 2]:
                rep[-s * d % 8, c] = add(("z", d, s, c), Z, s, 16, rep[-s * (d - 1) % 8, c])
    whole = {}
    for o in REP_AT:
        mine = [n for c in range(4) for n in rep[o, c]]
        whole[o] = mine + add(("cg", o), C, 1, 64, mine)
    cover = {}
    for i, ni, r, nr in TILES:
        needs = [n for k in range(i, i + ni) for h in (0, 1) for u in (0, 1) for n in img[IMG_AT[k], h, u]]
        needs += [n for k in range(r, r + nr) for n in whole[REP_AT[k]]]
        add(("tile", i, ni, r, nr), None, 0, ni * nr, needs)
        for k in range(i, i + ni):
            for m in range(r, r + nr):
                cover[k, m] = ("tile", i, ni, r, nr)
    img_tiles = lambda blocks: [cover[IMG_POS[o], m] for o in blocks for m in range(8)]
    rep_tiles = lambda blocks: [cover[k, REP_POS[o]] for o in blocks for k in range(16)]
    add("ig2", None, 0, 256, img_tiles([at(h, j, 2) for h in (0, 1) for j in JS]))
    for h in (0, 1):
        add(("ig1", h), None, 0, 256, img_tiles([at(h, j, s) for s in SIGNS for j in JS]))
    add("ig0", None, 0, 256, img_tiles([at(h, j, 0) for h in (0, 1) for j in JS]))
    for d in (4, 3, 2, 1, 0):
        add(("rg", d), None, 0, 256, rep_tiles([d] if d in (0, 4) else [d, 8 - d]))
    for d in (4, 3, 2, 1, 0):
        for o in (d, 8 - d) if d in (1, 2, 3) else (d,):
            add(("cr", o), C, 1, 64, [("rg", d)])
    for s in SIGNS:
        order = z_chunks(s)
        for c in order[:2]:
            add(("rz", 4, s, c), Z, s, 16, [("cr", 4)])
        for d in (3, 2, 1):
            for c in order[2:] + order[:2]:
                before = [] if d == 3 and c in order[2:] else [("rz", d + 1, s, c)]
                add(("rz", d, s, c), Z, s, 16, [("cr", s * d % 8)] + before)
    for h in (0, 1):
        p, q = h, 1 - h
        for s in SIGNS:
            for j in JS:
                add(("r1", h, s, 0, j), q, s, 16, ["ig2"])
                add(("r1", h, s, 1, j), q, s, 16, [("ig1", h)])
                add(("r1", h, s, 2, j), q, s, 16, [("ig1", h), ("r1", h, s, 0, j)])
        for n, s in enumerate(SIGNS):
            line = lambda j, u: ["ig0", ("r1", h, SIGNS[u], 2, j), ("r1", h, SIGNS[1 - u], 1, j)]
            add(("r2", h, s, 0), p, s, 16, line(2, n))
            add(("r2", h, s, 1), p, s, 16, line(s % 4, 1 - n))
            add(("r2", h, s, 2), p, s, 16, line(s % 4, n) + [("r2", h, s, 0)])
    add("loss", None, 0, 0, list(cover.values()))
    for d in (1, 2, 3):
        add(("lx", d), X, d, 2, ["loss"])
    for d in (1, 2, 3):
        add(("ly", d), Y, d, 2, [("lx", e) for e in (1, 2, 3)])
    add("out_rep", None, 0, 0, [("cr", 0)] + [("rz", 1, s, c) for s in SIGNS for c in range(4)])
    lines = [("r1", h, s, k, 0) for h in (0, 1) for s in SIGNS for k in (1, 2)]
    add("out_img", None, 0, 0, ["ig0"] + lines + [("r2", h, s, k) for h in (0, 1) for s in SIGNS for k in (1, 2)])
    add("out_loss", None, 0, 0, [("ly", d) for d in (1, 2, 3)])
    return steps


SENDS = ("g1", "g2", "g3", "g4", "z", "cg", "cr", "rz", "r1", "r2", "lx", "ly")

ORDER = [
    30, 61, 74, 75, 3, 0, 77, 1, 60, 62, 33, 31, 32, 39, 6, 9, 36, 63, 76, 8, 37, 38, 2, 88, 7, 34, 48, 65, 78, 5, 4,
    18, 15, 14, 49, 35, 44, 45, 19, 51, 64, 79, 50, 12, 13, 42, 43, 10, 66, 81, 11, 40, 41, 90, 67, 80, 89, 21, 20,
    96, 69, 26, 82, 54, 27, 52, 55, 17, 22, 24, 68, 25, 83, 57, 56, 70, 85, 47, 16, 71, 84, 53, 92, 91, 46, 23, 97,
    73, 86, 98, 58, 72, 29, 87, 59, 28, 94, 93, 99, 100, 95, 101, 103, 102, 108, 113, 104, 149, 161, 179, 191, 185,
    194, 152, 182, 197, 164, 167, 158, 155, 170, 188, 200, 135, 122, 136, 121, 109, 115, 114, 209, 211, 212, 210, 105,
    162, 150, 156, 168, 106, 201, 186, 123, 124, 192, 198, 138, 180, 183, 159, 137, 165, 110, 193, 181, 151, 117, 163,
    195, 153, 116, 189, 139, 126, 171, 107, 166, 140, 125, 187, 196, 154, 111, 213, 184, 199, 169, 118, 119, 214, 160,
    215, 112, 190, 202, 120, 172, 157, 127, 142, 128, 141, 130, 143, 173, 176, 203, 206, 129, 144, 218, 174, 207, 204,
    131, 146, 132, 145, 177, 134, 147, 175, 178, 205, 208, 133, 148, 217, 216,
]


def group_of(name):
    last = (name[0] == "r2" and name[3] > 0) or (name[0] == "rz" and name[1] == 1) or name[0] in ("lx", "ly")
    return name[0] if last else name


def my_coords():
    i, t = lax.axis_index("img"), lax.axis_index("txt")
    x, z_hi = lax.rem(t, 4), lax.div(t, 4)
    y, z_lo, c = lax.div(i, 4), lax.rem(lax.div(i, 2), 2), lax.rem(i, 2)
    return (x, y, z_hi * 2 + z_lo, c)


def device_at(co, axis, step):
    co = list(co)
    co[axis] = lax.rem(co[axis] + step + SIZES[axis], SIZES[axis])
    x, y, z, c = co
    return (y * 4 + lax.rem(z, 2) * 2 + c, lax.div(z, 2) * 4 + x)


def unit_rows(ref):
    wide = ref[...].astype(F32)
    inverse = lax.rsqrt(jnp.sum(wide * wide, axis=1, keepdims=True) + 1e-06)
    return wide * inverse, inverse


def project_back(grads, unit_wide, inverse):
    return inverse * (grads - unit_wide * jnp.sum(unit_wide * grads, axis=1, keepdims=True))


def kernel(
    img_ref, rep_ref, gimg_ref, grep_ref, loss_ref,
    own_img, own_rep, ibuf, rbuf, slopes, above, below, gr, ga1, gy,
    st_c, ld_c, st_z, ld_z, st1, ld1, st2, ld2, lb_s, lb_l, lw_s, lw_l,
    ssem, rsem, own_sem,
):
    me = my_coords()
    peers = [(X, 1), (X, -1), (X, 2), (Y, 1), (Y, -1), (Y, 2), (Z, 1), (Z, -1), (C, 1)]
    barrier = pltpu.get_barrier_semaphore()
    for axis, step in peers:
        pl.semaphore_signal(barrier, inc=1, device_id=device_at(me, axis, step), device_id_type=MESH)
    loads = [
        pltpu.make_async_copy(img_ref, own_img, own_sem.at[0]),
        pltpu.make_async_copy(rep_ref, own_rep, own_sem.at[1]),
    ]
    for load in loads:
        load.start()
    above[...] = jnp.zeros_like(above)
    below[...] = jnp.zeros_like(below)
    lb_s[...] = jnp.zeros_like(lb_s)
    for load in loads:
        load.wait()
    ibuf[0] = unit_rows(own_img)[0].astype(BF16)
    rbuf[0, 0] = unit_rows(own_rep)[0].astype(BF16)
    pl.semaphore_wait(barrier, len(peers))

    def quarter(n, count=1):
        return pl.ds(n * 16, count * 16)

    matched = jnp.logical_and(me[Y] == lax.div(me[Z], 2), me[X] == lax.rem(me[Z], 2) * 2 + me[C])
    aside = jnp.where(matched, 0, 1 << 20)
    row_in = lax.broadcasted_iota(jnp.int32, (64, 1), 0)
    col_in = lax.broadcasted_iota(jnp.int32, (1, 128), 1)

    def tile(i, ni, r, nr):
        m = ni * 64
        lhs = ibuf[i : i + ni].reshape(m, D)
        rhs = rbuf[r : r + nr].reshape(nr * 128, D)
        dots = lax.dot_general(lhs, rhs, (((1,), (1,)), ((), ())), preferred_element_type=F32)
        row_ids = []
        for dx, dy in IMG_AT[i : i + ni]:
            block = lax.rem(me[Y] + dy, 4) * 4 + lax.rem(me[X] + dx, 4)
            row_ids.append(block * 64 + aside + row_in)
        row_ids = jnp.concatenate(row_ids, axis=0)
        high = above[i : i + ni].reshape(m, 128)
        low = below[i : i + ni].reshape(m, 128)
        for k in range(nr):
            bz = lax.rem(me[Z] + REP_AT[r + k], 8) * 2
            mine, other = (bz + me[C]) * 64, (bz + 1 - me[C]) * 64
            col_ids = jnp.where(col_in < 64, mine + col_in, other + col_in - 64)
            sign = jnp.where(row_ids == col_ids, -1.0, 1.0)
            bits = (dots[:, k * 128 : k * 128 + 128] * (logit_scale * LOG2E) + logit_bias * LOG2E) * sign
            e = jnp.exp2(-jnp.abs(bits))
            one_e = 1.0 + e
            inverse = 1.0 / one_e
            slope = jnp.where(bits >= 0, inverse, e * inverse) * sign
            slopes[i : i + ni, :, (r + k) * 128 : (r + k) * 128 + 128] = slope.astype(BF16).reshape(ni, 64, 128)
            high = high + jnp.maximum(bits, 0.0)
            low = low * one_e + e
        above[i : i + ni] = high.reshape(ni, 64, 128)
        below[i : i + ni] = low.reshape(ni, 64, 128)

    def img_terms(pieces):
        lhs = jnp.concatenate([slopes[IMG_POS[at(*n)], quarter(2 * n[0], 2)] for n in pieces], axis=0)
        return logit_scale * jnp.dot(lhs, rbuf[...].reshape(1024, D), preferred_element_type=F32)

    def rep_terms(offsets):
        cols = [slopes[:, :, REP_POS[o] * 128 : REP_POS[o] * 128 + 128].reshape(1024, 128) for o in offsets]
        out = logit_scale * lax.dot_general(
            jnp.concatenate(cols, axis=1) if len(cols) > 1 else cols[0], ibuf[...].reshape(1024, D), (((0,), (0,)), ((), ())),
            preferred_element_type=F32,
        )
        for n, o in enumerate(offsets):
            gr[REP_POS[o]] = out[n * 128 : n * 128 + 64]
            st_c[REP_POS[o]] = out[n * 128 + 64 : n * 128 + 128].astype(BF16)

    def far_terms():
        out = img_terms([(h, j, 2) for h in (0, 1) for j in JS])
        for h in (0, 1):
            for k in range(4):
                for n in (0, 1):
                    base = (h * 4 + k) * 32 + n * 16
                    st1[h, n, 0, k] = out[base : base + 16].astype(BF16)

    def near_terms(h):
        out = img_terms([(h, j, s) for s in SIGNS for j in JS])
        for n in (0, 1):
            for k in range(4):
                base = (n * 4 + k) * 32
                quarters = [out[base : base + 16], out[base + 16 : base + 32]]
                st1[h, n, 1, k] = quarters[1 - n].astype(BF16)
                ga1[h, n, k] = quarters[n]

    def line_terms():
        out = img_terms([(h, j, 0) for h in (0, 1) for j in JS])
        for h in (0, 1):
            for k in range(4):
                gy[h, k] = out[(h * 4 + k) * 32 : (h * 4 + k) * 32 + 32]

    def line_sum(h, j, u):
        k = JS.index(j)
        total = gy[h, k, quarter(u)] + ld1[h, u, 2, k].astype(F32)
        return total + ld1[h, 1 - u, 1, k].astype(F32)

    def paired(o, c):
        return gr[REP_POS[o % 8], quarter(c)] + ld_c[REP_POS[o % 8], quarter(c)].astype(F32)

    def losses():
        for k in range(8):
            wide = above[2 * k : 2 * k + 2] * LN2 + jnp.log1p(below[2 * k : 2 * k + 2])
            line = jnp.sum(wide.reshape(128, 128).T, axis=0, keepdims=True)
            for n in (0, 1):
                dx, dy = IMG_AT[2 * k + n]
                lb_s[dx, dy : dy + 1, :] = line if n == 0 else pltpu.roll(line, 64, 1)

    def x_losses():
        lw_s[...] = lb_s[0] + lb_l[1] + lb_l[2] + lb_l[3]

    def out_rep():
        parts = [paired(0, c) + ld_z[0, 0, c].astype(F32) + ld_z[1, 0, c].astype(F32) for c in range(4)]
        unit, inverse = unit_rows(own_rep)
        grep_ref[...] = project_back(jnp.concatenate(parts, axis=0), unit, inverse)

    def out_img():
        parts = [
            line_sum(h, 0, u) + ld2[h, u, 2].astype(F32) + ld2[h, 1 - u, 1].astype(F32)
            for h in (0, 1)
            for u in (0, 1)
        ]
        unit, inverse = unit_rows(own_img)
        gimg_ref[...] = project_back(jnp.concatenate(parts, axis=0), unit, inverse)

    def out_loss():
        loss = lw_s[0:1, :]
        for d in (1, 2, 3):
            loss = loss + lw_l[d, d : d + 1, :]
        loss_ref[...] = jnp.broadcast_to(loss, loss_ref.shape)

    compute = {
        "tile": tile, "ig2": far_terms, "ig1": near_terms, "ig0": line_terms,
        "rg": lambda d: rep_terms([d] if d in (0, 4) else [d, 8 - d]),
        "loss": losses, "out_rep": out_rep, "out_img": out_img, "out_loss": out_loss,
    }

    def img_ends(o, part, axis, s):
        return ibuf.at[IMG_POS[o], part], ibuf.at[IMG_POS[shift(o, axis, -s)], part]

    def ends(name):
        kind, a = name[0], name[1:]
        if kind == "g1":
            h, s, u = a
            return img_ends((0, 0), quarter(2 * h + u), h, s)
        if kind == "g2":
            h, s = a
            return img_ends(shift((0, 0), h, -s), quarter(2 * h + SIGNS.index(s)), h, s)
        if kind == "g3":
            h, s, j, u = a
            return img_ends(at(h, j, 0), quarter(2 * h + u), 1 - h, s)
        if kind == "g4":
            h, s, j = a
            return img_ends(at(h, j, -s), quarter(2 * h + SIGNS.index(s)), 1 - h, s)
        if kind == "z":
            d, s, c = a
            return (
                rbuf.at[REP_POS[-s * (d - 1) % 8], 0, quarter(c)],
                rbuf.at[REP_POS[-s * d % 8], 0, quarter(c)],
            )
        if kind == "cg":
            return rbuf.at[REP_POS[a[0]], 0], rbuf.at[REP_POS[a[0]], 1]
        if kind == "cr":
            return st_c.at[REP_POS[a[0]]], ld_c.at[REP_POS[a[0]]]
        if kind == "rz":
            d, s, c = a
            return st_z.at[SIGNS.index(s), d - 1, c], ld_z.at[SIGNS.index(s), d - 1, c]
        if kind == "r1":
            h, s, slot, j = a
            where = (h, SIGNS.index(s), slot, JS.index(j))
            return st1.at[where], ld1.at[where]
        if kind == "r2":
            h, s, slot = a
            return st2.at[h, SIGNS.index(s), slot], ld2.at[h, SIGNS.index(s), slot]
        if kind == "lx":
            return lb_s.at[a[0]], lb_l.at[a[0]]
        return lw_s, lw_l.at[a[0]]

    def prepare(name):
        kind, a = name[0], name[1:]
        if kind == "rz":
            d, s, c = a
            n = SIGNS.index(s)
            term = paired(s * d, c)
            if d < 3 or (d == 3 and c in z_chunks(s)[:2]):
                term = term + ld_z[n, d, c].astype(F32)
            st_z[n, d - 1, c] = term.astype(BF16)
        if kind == "r1" and a[2] == 2:
            h, s, _, j = a
            n, k = SIGNS.index(s), JS.index(j)
            st1[h, n, 2, k] = (ga1[h, n, k] + ld1[h, n, 0, k].astype(F32)).astype(BF16)
        if kind == "r2":
            h, s, slot = a
            n = SIGNS.index(s)
            term = line_sum(h, 2 if slot == 0 else s % 4, 1 - n if slot == 1 else n)
            if slot == 2:
                term = term + ld2[h, n, 0].astype(F32)
            st2[h, n, slot] = term.astype(BF16)
        if name == ("ly", 1):
            x_losses()

    steps = plan()
    copies = {}
    together = {
        "r2": ibuf.at[pl.ds(0, 2)], "rz": ibuf.at[pl.ds(0, 2)], "lx": lb_s.at[pl.ds(1, 3)], "ly": lw_l.at[pl.ds(1, 3)],
    }
    landing = {}
    for name, axis, step, _, _ in steps:
        if axis is not None:
            k = landing.setdefault(group_of(name), len(landing))
            src, dst = ends(name)
            copies[name] = pltpu.make_async_remote_copy(
                src, dst, ssem.at[SENDS.index(name[0])], rsem.at[k], device_id=device_at(me, axis, step), device_id_type=MESH
            )
    arrived = set()
    for n in ORDER:
        name, axis, _, _, needs = steps[n]
        for need in needs:
            group = group_of(need)
            if need in copies and group not in arrived:
                copy = copies[need]
                if group in together:
                    copy = pltpu.make_async_remote_copy(
                        together[group], together[group], ssem.at[0], rsem.at[landing[group]],
                        device_id=device_at(me, C, 1), device_id_type=MESH,
                    )
                copy.wait_recv()
                arrived.add(group)
        if axis is None:
            args = () if isinstance(name, str) else name[1:]
            compute[name if isinstance(name, str) else name[0]](*args)
        else:
            prepare(name)
            copies[name].start()
    sent = {
        "g1": ibuf.at[pl.ds(0, 2)], "g2": ibuf.at[pl.ds(0, 1)], "g3": ibuf.at[pl.ds(0, 8)], "g4": ibuf.at[pl.ds(0, 4)],
        "z": rbuf.at[pl.ds(0, 7), 0], "cg": rbuf.at[:, 0], "cr": st_c, "rz": rbuf.at[pl.ds(0, 7), 0],
        "r1": st1, "r2": st2, "lx": lb_s.at[pl.ds(1, 3)], "ly": lw_l.at[pl.ds(1, 3)],
    }
    for n, kind in enumerate(SENDS):
        pltpu.make_async_remote_copy(
            sent[kind], sent[kind], ssem.at[n], rsem.at[0], device_id=device_at(me, C, 1), device_id_type=MESH
        ).wait_send()


def finish(gimg, grep, loss, out_img, out_rep, out_loss, sem):
    stores = [pltpu.make_async_copy(gimg, out_img, sem.at[0]), pltpu.make_async_copy(grep, out_rep, sem.at[1])]
    for store in stores:
        store.start()
    out_loss[...] = loss[0, :64]
    for store in stores:
        store.wait()


LANDINGS = len({group_of(step[0]) for step in plan() if step[1] is not None})


def on_device(image_emb, report_emb):
    vmem = pl.BlockSpec(memory_space=pltpu.VMEM)
    hbm = pl.BlockSpec(memory_space=pl.ANY)
    sums = (
        jax.ShapeDtypeStruct((64, D), F32),
        jax.ShapeDtypeStruct((64, D), F32),
        jax.ShapeDtypeStruct((8, 128), F32),
    )
    gimg, grep, loss = pl.pallas_call(
        kernel,
        out_shape=(pltpu.VMEM((64, D), F32), pltpu.VMEM((64, D), F32), pltpu.VMEM((8, 128), F32)),
        in_specs=[pl.BlockSpec(memory_space=pltpu.HBM)] * 2,
        out_specs=(vmem, vmem, vmem),
        scratch_shapes=[
            pltpu.VMEM((64, D), BF16),
            pltpu.VMEM((64, D), BF16),
            pltpu.VMEM((16, 64, D), BF16),
            pltpu.VMEM((8, 2, 64, D), BF16),
            pltpu.VMEM((16, 64, 1024), BF16),
            pltpu.VMEM((16, 64, 128), F32),
            pltpu.VMEM((16, 64, 128), F32),
            pltpu.VMEM((8, 64, D), F32),
            pltpu.VMEM((2, 2, 4, 16, D), F32),
            pltpu.VMEM((2, 4, 32, D), F32),
            pltpu.VMEM((8, 64, D), BF16),
            pltpu.VMEM((8, 64, D), BF16),
            pltpu.VMEM((2, 4, 4, 16, D), BF16),
            pltpu.VMEM((2, 4, 4, 16, D), BF16),
            pltpu.VMEM((2, 2, 3, 4, 16, D), BF16),
            pltpu.VMEM((2, 2, 3, 4, 16, D), BF16),
            pltpu.VMEM((2, 2, 3, 16, D), BF16),
            pltpu.VMEM((2, 2, 3, 16, D), BF16),
            pltpu.VMEM((4, 8, 128), F32),
            pltpu.VMEM((4, 8, 128), F32),
            pltpu.VMEM((8, 128), F32),
            pltpu.VMEM((4, 8, 128), F32),
            pltpu.SemaphoreType.DMA((len(SENDS),)),
            pltpu.SemaphoreType.DMA((LANDINGS,)),
            pltpu.SemaphoreType.DMA((2,)),
        ],
        compiler_params=pltpu.CompilerParams(
            collective_id=0, has_side_effects=True, vmem_limit_bytes=40 * 2**20
        ),
        cost_estimate=pl.CostEstimate(
            flops=3 * 2 * 1024 * 1024 * D, bytes_accessed=900000, transcendentals=3 * 1024 * 1024
        ),
    )(pltpu.with_memory_space_constraint(image_emb, pltpu.HBM), pltpu.with_memory_space_constraint(report_emb, pltpu.HBM))
    return pl.pallas_call(
        finish,
        out_shape=sums[:2] + (jax.ShapeDtypeStruct((64,), F32),),
        in_specs=[vmem, vmem, vmem],
        out_specs=(hbm, hbm, vmem),
        scratch_shapes=[pltpu.SemaphoreType.DMA((2,))],
        compiler_params=pltpu.CompilerParams(vmem_limit_bytes=8 * 2**20),
    )(gimg, grep, loss)


def solution(mesh):
    in_specs = (P(("img", "txt"), None), P(("txt", "img"), None))
    out_specs = (P(("img", "txt"), None), P(("txt", "img"), None), P(("img", "txt")))
    return jax.shard_map(
        on_device, mesh=mesh, in_specs=in_specs, out_specs=out_specs, check_vma=False
    )
```
